256 devices in a mesh: outer: 8 (over y, z_hi), inner: 32 (over z_lo, x, core).
Axes of the slice: x: 4, y: 4, z: 8 (z_hi: 2, z_lo: 4; z = z_hi * 4 + z_lo), core: 2. Of those that a mesh axis runs over, the one named last changes fastest.
Arguments:
- query: bfloat16 [32768, 24, 128], P(('outer', 'inner')), may hold values from -6 to 6
- key: bfloat16 [32768, 4, 128], P(('outer', 'inner')), may hold values from -6 to 6
- value: bfloat16 [32768, 4, 128], P(('outer', 'inner')), may hold values from -0.625 to 0.625
- output: bfloat16 [32768, 24, 128], P(('outer', 'inner')), may hold values from -0.625 to 0.625
- grad_output: bfloat16 [32768, 24, 128], P(('outer', 'inner')), may hold values from -6 to 6
- lse: float32 [24, 32768], P(None, ('outer', 'inner')), may hold values from 2 to 5
- doc_starts: int32 [24], replicated, may hold values from 0 to 31232, as said below
Outputs:
- grad_query: bfloat16 [32768, 24, 128], P(('outer', 'inner'))
- grad_key: bfloat16 [32768, 4, 128], P(('outer', 'inner'))
- grad_value: bfloat16 [32768, 4, 128], P(('outer', 'inner'))
The draws below stay inside these ranges and needn't reach their ends.
Inputs may be any that keep to these rules, and one draw needn't show every extreme that they name: `doc_starts`: strictly increasing, the first entry 0. Window w holds positions w * 4096 to (w + 1) * 4096 - 1. Entries 3w + 1 and 3w + 2 lie inside window w; for w >= 1, entry 3w lies within the last 1536 positions of window w - 1, and entry 3w + 1 is at most w * 4096 + 4096 // 4. No document is longer than 2560 tokens.
All inputs are finite; a program needn't handle non-finite values.
Results may differ from the reference program's by a relative error of at most 0.02.
Values may be sent and summed in bfloat16 or wider, within the bound.
A program may use at most 128 MiB of HBM per device.

```python
import math
import jax
import jax.numpy as jnp
from jax import lax

HEADS = 24
KV_HEADS = 4
HEAD_DIM = 128
GROUP = 6
TOK_DEV = 128
BLOCK = 64
WINDOW = 4096
TOKENS = 32768
DOCS = 24
N_OUTER = 8
N_INNER = 32


def draw_doc_starts(key, part):
    key = jax.random.fold_in(key, 11)
    subkeys = jax.random.split(key, 3)
    windows = jnp.arange(N_OUTER, dtype=jnp.int32)
    reach_back = jax.random.randint(subkeys[0], (N_OUTER,), WINDOW // 4, 3 * WINDOW // 8, dtype=jnp.int32)
    reach_back = jnp.where(windows == 0, 0, reach_back)
    lead_in = jax.random.randint(subkeys[1], (N_OUTER,), WINDOW // 8, WINDOW // 4 + 1, dtype=jnp.int32)
    second_start = jax.random.randint(subkeys[2], (N_OUTER,), 1, WINDOW // 8 + 1, dtype=jnp.int32)
    second_start = jnp.where(windows == N_OUTER - 1, WINDOW // 8, second_start)
    window_base = windows * WINDOW
    starts = jnp.stack([window_base - reach_back, window_base + lead_in, window_base + WINDOW // 2 + second_start], axis=1)
    return starts.reshape(DOCS).astype(jnp.int32)


def levels(rng, shape, shards, low, high):
    def one(axis_at, shards_of):
        steps = jax.random.uniform(jax.random.fold_in(jax.random.fold_in(rng, 6), axis_at), (shards_of,), jnp.float32, low / len(shards), high / len(shards))
        return jnp.repeat(jnp.exp(steps), shape[axis_at] // shards_of).reshape((-1,) + (1,) * (len(shape) - axis_at - 1))

    factor_of = one(*shards[0])
    for cut in shards[1:]:
        factor_of = factor_of * one(*cut)
    return factor_of


def centred(own_key, shape, deviation, limit, shards=(), kind=jnp.bfloat16):
    values = deviation * jax.random.normal(own_key, shape, jnp.float32)
    if shards:
        values = values * levels(own_key, shape, shards, -0.22, 0.18)
    return jnp.clip(values, -limit, limit).astype(kind)


def setup_inputs(seed: int = 0) -> dict:
    streams_of = jax.random.split(jax.random.key(seed), 8)
    return {
        "query": centred(streams_of[0], (TOKENS, HEADS, HEAD_DIM), 1.0, 6.0, ((0, 256),)),
        "key": centred(streams_of[1], (TOKENS, KV_HEADS, HEAD_DIM), 1.0, 6.0, ((0, 256),)),
        "value": centred(streams_of[2], (TOKENS, KV_HEADS, HEAD_DIM), 0.1, 0.625, ((0, 256),)),
        "output": centred(streams_of[3], (TOKENS, HEADS, HEAD_DIM), 0.1, 0.625, ((0, 256),)),
        "grad_output": centred(streams_of[4], (TOKENS, HEADS, HEAD_DIM), 1.0, 6.0, ((0, 256),)),
        "lse": jnp.clip(2.0 + 3.0 * jax.random.uniform(streams_of[5], (HEADS, TOKENS), jnp.float32) ** levels(streams_of[5], (HEADS, TOKENS), ((1, 256),), -0.2, 0.2), 2.0, 5.0),
        "doc_starts": draw_doc_starts(jax.random.fold_in(streams_of[7], 71), 0),
    }


def round_low(values):
    rounded = values.astype(jnp.bfloat16)
    rounded = lax.optimization_barrier(rounded)
    return rounded.astype(jnp.float32)

def stored_rows():
    sequence = jnp.arange(TOKENS, dtype=jnp.int32)
    window = sequence // WINDOW
    within = sequence % WINDOW
    block_no = within // BLOCK
    offset = within % BLOCK
    device = jnp.where(block_no < N_INNER, block_no, 2 * N_INNER - 1 - block_no)
    upper_half = (block_no >= N_INNER).astype(jnp.int32)
    return window * WINDOW + device * TOK_DEV + upper_half * BLOCK + offset

def block_terms(query_rows, grad_rows, lse_rows, delta_rows, query_pos, query_doc, key_rows, value_rows, key_pos, key_doc, score_scale):
    scores = jnp.einsum('qhgd,khd->hgqk', query_rows, key_rows) * score_scale
    allowed = (key_pos[None, :] <= query_pos[:, None]) & (key_doc[None, :] == query_doc[:, None])
    weights = jnp.where(allowed, jnp.exp(scores - lse_rows[..., None]), 0.0)
    grad_weights = jnp.einsum('qhgd,khd->hgqk', grad_rows, value_rows)
    grad_scores = weights * (grad_weights - delta_rows[..., None])
    weights_low = round_low(weights)
    grad_scores_low = round_low(grad_scores)
    query_part = jnp.einsum('hgqk,khd->qhgd', grad_scores_low, key_rows)
    key_part = jnp.einsum('hgqk,qhgd->khd', grad_scores_low, query_rows)
    value_part = jnp.einsum('hgqk,qhgd->khd', weights_low, grad_rows)
    return (query_part, key_part, value_part)

def reference(query, key, value, output, grad_output, lse, doc_starts):
    score_scale = 1.0 / math.sqrt(HEAD_DIM)
    rows_of = stored_rows()
    query_seq = query[rows_of].astype(jnp.float32).reshape(TOKENS, KV_HEADS, GROUP, HEAD_DIM)
    grad_seq = grad_output[rows_of].astype(jnp.float32).reshape(TOKENS, KV_HEADS, GROUP, HEAD_DIM)
    output_seq = output[rows_of].astype(jnp.float32).reshape(TOKENS, KV_HEADS, GROUP, HEAD_DIM)
    delta = jnp.einsum('phgd,phgd->hgp', grad_seq, output_seq)
    lse_seq = lse[:, rows_of].astype(jnp.float32).reshape(KV_HEADS, GROUP, TOKENS)
    positions = jnp.arange(TOKENS + WINDOW, dtype=jnp.int32) - WINDOW
    doc_ids = lax.optimization_barrier(jnp.sum((doc_starts[None, :] <= positions[:, None]).astype(jnp.int32), axis=1)) - 1
    padding = jnp.zeros((WINDOW, KV_HEADS, HEAD_DIM), jnp.float32)
    key_pad = jnp.concatenate([padding, key[rows_of].astype(jnp.float32)], axis=0)
    value_pad = jnp.concatenate([padding, value[rows_of].astype(jnp.float32)], axis=0)
    span = 5 * WINDOW // 8 + BLOCK

    def per_device(totals, flat):
        key_total, value_total = totals
        window = flat // N_INNER
        device = flat % N_INNER
        frame_key = jnp.zeros((2 * WINDOW, KV_HEADS, HEAD_DIM), jnp.float32)
        frame_value = jnp.zeros((2 * WINDOW, KV_HEADS, HEAD_DIM), jnp.float32)
        query_grads = []
        for upper_half in (0, 1):
            block_no = device if upper_half == 0 else 2 * N_INNER - 1 - device
            first = (window * WINDOW + block_no * BLOCK).astype(jnp.int32)
            query_rows = lax.dynamic_slice_in_dim(query_seq, first, BLOCK, 0)
            grad_rows = lax.dynamic_slice_in_dim(grad_seq, first, BLOCK, 0)
            lse_rows = lax.dynamic_slice_in_dim(lse_seq, first, BLOCK, 2)
            delta_rows = lax.dynamic_slice_in_dim(delta, first, BLOCK, 2)
            query_pos = first + jnp.arange(BLOCK, dtype=jnp.int32)
            query_doc = lax.dynamic_slice_in_dim(doc_ids, first + WINDOW, BLOCK, 0)
            key_from = (first + BLOCK + WINDOW - span).astype(jnp.int32)
            key_rows = lax.dynamic_slice_in_dim(key_pad, key_from, span, 0)
            value_rows = lax.dynamic_slice_in_dim(value_pad, key_from, span, 0)
            key_pos = lax.dynamic_slice_in_dim(positions, key_from, span, 0)
            key_doc = lax.dynamic_slice_in_dim(doc_ids, key_from, span, 0)
            query_part, key_part, value_part = block_terms(query_rows, grad_rows, lse_rows, delta_rows, query_pos, query_doc, key_rows, value_rows, key_pos, key_doc, score_scale)
            query_grads.append((query_part * score_scale).astype(jnp.bfloat16))
            into = (key_from - window * WINDOW).astype(jnp.int32)
            frame_key = lax.dynamic_update_slice_in_dim(frame_key, lax.dynamic_slice_in_dim(frame_key, into, span, 0) + key_part * score_scale, into, 0)
            frame_value = lax.dynamic_update_slice_in_dim(frame_value, lax.dynamic_slice_in_dim(frame_value, into, span, 0) + value_part, into, 0)
        anchor = (window * WINDOW).astype(jnp.int32)
        key_total = lax.dynamic_update_slice_in_dim(key_total, lax.dynamic_slice_in_dim(key_total, anchor, 2 * WINDOW, 0) + round_low(frame_key), anchor, 0)
        value_total = lax.dynamic_update_slice_in_dim(value_total, lax.dynamic_slice_in_dim(value_total, anchor, 2 * WINDOW, 0) + round_low(frame_value), anchor, 0)
        return ((key_total, value_total), jnp.stack(query_grads))
    start_totals = (jnp.zeros((TOKENS + WINDOW, KV_HEADS, HEAD_DIM), jnp.float32), jnp.zeros((TOKENS + WINDOW, KV_HEADS, HEAD_DIM), jnp.float32))
    totals, query_blocks = lax.scan(per_device, start_totals, jnp.arange(N_OUTER * N_INNER, dtype=jnp.int32))
    grad_query = query_blocks.reshape(TOKENS, HEADS, HEAD_DIM)
    key_seq = totals[0][WINDOW:].astype(jnp.bfloat16)
    value_seq = totals[1][WINDOW:].astype(jnp.bfloat16)
    grad_key = jnp.zeros((TOKENS, KV_HEADS, HEAD_DIM), jnp.bfloat16).at[rows_of].set(key_seq)
    grad_value = jnp.zeros((TOKENS, KV_HEADS, HEAD_DIM), jnp.bfloat16).at[rows_of].set(value_seq)
    return (grad_query, grad_key, grad_value)
```

```python
import math

import jax
import jax.numpy as jnp
from jax import lax
from jax.experimental import pallas as pl
from jax.experimental.pallas import tpu as pltpu
from jax.sharding import PartitionSpec as P

MESH = pl.DeviceIdType.MESH
ZS, XS = 4, 4
KV, GROUP, DIM, BLK = 4, 6, 128, 64
ROWS = GROUP * BLK
WINDOWS = 8
WIN_BLOCKS = 64
WIN_ROWS = WIN_BLOCKS * BLK
PAD_PAIRS, PRIOR_PAIRS = 2, 12
BASE_PAIRS = PAD_PAIRS + PRIOR_PAIRS
PAIRS = BASE_PAIRS + WIN_BLOCKS // 2
KEY_ROWS = PAIRS * 2 * BLK
BASE_ROW = BASE_PAIRS * 2 * BLK
TILE = 256
SCALE = 1.0 / math.sqrt(DIM)
LOG2E = math.log2(math.e)

NEED = {
    0: (0, 4, 5, 2, 6, 3, 7, 8, 9, 10),
    1: (1, 5, 0, 2, 6, 3, 7, 8, 9, 10),
    2: (2, 6, 1, 3, 7, 0),
    3: (3, 7, 2, 1, 0),
}
PRIOR_FROM = (0, 1, 2)
PRIOR_TO = (0, 1)


def owner_z(gid):
    return gid % 4


def place():
    inner = lax.axis_index("inner")
    return lax.axis_index("outer"), inner // (2 * XS), (inner // 2) % XS, inner % 2


def device(window, z, x, core):
    return {"outer": window, "inner": (z * XS + x) * 2 + core}


def group_slot(gid, core):
    z = owner_z(gid)
    if gid < 4:
        return BASE_PAIRS + 4 * z, core
    if gid < 8:
        return BASE_PAIRS + 28 - 4 * z, 1 - core
    return PAD_PAIRS + 8 - 4 * z, 1 - core


def group_of(ref, gid, core):
    pair, parity = group_slot(gid, core)
    return ref.at[:, pl.ds(pair, 4), parity]


def block_of(ref, half, z, x, core):
    if half == 0:
        return ref.at[:, BASE_PAIRS + 4 * z + x, core]
    return ref.at[:, BASE_PAIRS + 31 - 4 * z - x, 1 - core]


def has_next(window, z):
    return (window < WINDOWS - 1) & (z <= 2)


def has_previous(window, z):
    return (window > 0) & (z <= 1)


def greet(window, z, x, core):
    barrier = pltpu.get_barrier_semaphore()

    def signal(*where):
        pl.semaphore_signal(barrier, inc=1, device_id=device(*where), device_id_type=MESH)

    for step in range(1, XS):
        signal(window, z, (x + step) % XS, core)
    for step in range(1, ZS):
        signal(window, (z + step) % ZS, x, core)
    signal(window, z, x, 1 - core)

    @pl.when(has_next(window, z))
    def _():
        for other in PRIOR_TO:
            signal(window + 1, other, x, core)

    @pl.when(has_previous(window, z))
    def _():
        for other in PRIOR_FROM:
            signal(window - 1, other, x, core)

    count = 7 + jnp.where(has_next(window, z), 2, 0) + jnp.where(has_previous(window, z), 3, 0)
    pl.semaphore_wait(barrier, count)


def remote(src, dst, send, recv, where):
    return pltpu.make_async_remote_copy(
        src_ref=src, dst_ref=dst, send_sem=send, recv_sem=recv, device_id=where, device_id_type=MESH
    )


def spread_kernel(
    kv_src, qd_src, ld_src, kv, qd, ld,
    kv_send, kv_recv, qd_send, qd_recv, ld_send, ld_recv,
    z_send, z_recv, next_send, next_recv, core_send, core_recv, own_sem,
):
    window, z, x, core = place()
    greet(window, z, x, core)

    def kv_copy(step, half):
        to = (x + step) % XS
        return remote(
            kv_src.at[to, :, half], block_of(kv, half, z, x, core),
            kv_send.at[step - 1, half], kv_recv.at[step - 1, half], device(window, z, to, core),
        )

    def kv_arrival(step, half):
        came = (x - step + XS) % XS
        return remote(
            kv_src.at[came, :, half], block_of(kv, half, z, came, core),
            kv_send.at[step - 1, half], kv_recv.at[step - 1, half], device(window, z, came, core),
        )

    def wide_copy(src, dst, send, recv, step):
        to = (x + step) % XS
        return remote(src.at[to], dst.at[x], send.at[step - 1], recv.at[step - 1], device(window, z, to, core))

    def wide_arrival(src, dst, send, recv, step):
        came = (x - step + XS) % XS
        return remote(
            src.at[came], dst.at[came], send.at[step - 1], recv.at[step - 1], device(window, z, came, core)
        )

    for step in (2, 1, 3):
        for half in (0, 1):
            kv_copy(step, half).start()
    own = [
        pltpu.make_async_copy(kv_src.at[x, :, half], block_of(kv, half, z, x, core), own_sem.at[half])
        for half in (0, 1)
    ]
    own += [
        pltpu.make_async_copy(qd_src.at[x], qd.at[x], own_sem.at[2]),
        pltpu.make_async_copy(ld_src.at[x], ld.at[x], own_sem.at[3]),
    ]
    for copy in own:
        copy.start()
    for step in (2, 1, 3):
        wide_copy(ld_src, ld, ld_send, ld_recv, step).start()
        wide_copy(qd_src, qd, qd_send, qd_recv, step).start()
    for copy in own:
        copy.wait()
    for step in (2, 1, 3):
        for half in (0, 1):
            kv_arrival(step, half).wait_recv()

    def z_copy(gid, to):
        piece = group_of(kv, gid, core)
        return remote(
            piece, piece, z_send.at[to, gid // 4], z_recv.at[gid], device(window, to, x, core)
        )

    def next_copy(gid, to):
        return remote(
            group_of(kv, gid - 4, core), group_of(kv, gid, core),
            next_send.at[to], next_recv.at[gid - 8], device(window + 1, to, x, core),
        )

    def next_arrival(gid):
        piece = group_of(kv, gid, core)
        return remote(piece, piece, next_send.at[0], next_recv.at[gid - 8], device(window, z, x, 1 - core))

    def core_copy(gid):
        piece = group_of(kv, gid, core)
        return remote(piece, piece, core_send.at[gid], core_recv.at[gid], device(window, z, x, 1 - core))

    def core_arrival(gid):
        piece = group_of(kv, gid, 1 - core)
        return remote(piece, piece, core_send.at[gid], core_recv.at[gid], device(window, z, x, 1 - core))

    def level(at):
        mine = (at, at + 4)
        near = [gid for gid in NEED[at] if gid < 8 and gid not in mine]
        far = [gid for gid in NEED[at] if gid >= 8]
        sends = [
            (gid, to) for to in (0, 3, 1, 2) for gid in mine if to != at and gid in NEED[to]
        ]
        for gid, to in sends:
            z_copy(gid, to).start()
        if at in PRIOR_FROM:

            @pl.when(window < WINDOWS - 1)
            def _():
                for to in PRIOR_TO:
                    next_copy(at + 8, to).start()

        for gid in mine:
            core_copy(gid).start()
        for gid in near:
            z_copy(gid, (owner_z(gid))).wait_recv()
            core_copy(gid).start()
        if far:

            @pl.when(window > 0)
            def _():
                for gid in far:
                    next_arrival(gid).wait_recv()
                    core_copy(gid).start()
                for gid in far:
                    core_arrival(gid).wait_recv()
                    core_copy(gid).wait_send()

        for gid in (*mine, *near):
            core_arrival(gid).wait_recv()
            core_copy(gid).wait_send()
        for gid, to in sends:
            z_copy(gid, to).wait_send()
        if at in PRIOR_FROM:

            @pl.when(window < WINDOWS - 1)
            def _():
                for to in PRIOR_TO:
                    next_copy(at + 8, to).wait_send()

    for at in range(ZS):
        pl.when(z == at)(lambda at=at: level(at))

    for step in (1, 2, 3):
        for half in (0, 1):
            kv_copy(step, half).wait_send()
        wide_arrival(ld_src, ld, ld_send, ld_recv, step).wait_recv()
        wide_arrival(qd_src, qd, qd_send, qd_recv, step).wait_recv()
        wide_copy(ld_src, ld, ld_send, ld_recv, step).wait_send()
        wide_copy(qd_src, qd, qd_send, qd_recv, step).wait_send()


def spread(kv_src, qd_src, ld_src):
    dma = pltpu.SemaphoreType.DMA
    anywhere = pl.BlockSpec(memory_space=pl.ANY)
    return pl.pallas_call(
        spread_kernel,
        out_shape=(
            jax.ShapeDtypeStruct((2, PAIRS, 2, BLK, DIM), jnp.bfloat16),
            jax.ShapeDtypeStruct(qd_src.shape, jnp.bfloat16),
            jax.ShapeDtypeStruct(ld_src.shape, jnp.float32),
        ),
        in_specs=[anywhere] * 3,
        out_specs=[anywhere] * 3,
        scratch_shapes=[
            dma((3, 2)), dma((3, 2)), dma((3,)), dma((3,)), dma((3,)), dma((3,)),
            dma((ZS, 2)), dma((8,)), dma((2,)), dma((3,)), dma((11,)), dma((11,)), dma((4,)),
        ],
        compiler_params=pltpu.CompilerParams(collective_id=0, has_side_effects=True),
        name="spread",
    )(kv_src, qd_src, ld_src)


def grads_kernel(info, starts, qd, ld, kv_hbm, dq, parts, kv, totals, dq_t, kv_sem):
    src, half = pl.program_id(0), pl.program_id(1)
    window, z, core = info[0], info[1], info[2]

    @pl.when((src == 0) & (half == 0))
    def _():
        load = pltpu.make_async_copy(kv_hbm, kv, kv_sem)
        load.start()
        totals[...] = jnp.zeros_like(totals)
        load.wait()

        def clear(first, blocks):
            kv[:, pl.ds(first * BLK, blocks * BLK), :] = jnp.zeros((2, blocks * BLK, DIM), jnp.bfloat16)

        clear(0, 2 * PAD_PAIRS)
        pl.when((z >= 2) | (window == 0))(lambda: clear(2 * PAD_PAIRS, 2 * PRIOR_PAIRS))
        pl.when(z == 0)(lambda: clear(2 * BASE_PAIRS + 8, 8))

    low = 8 * z + 2 * src + core
    block = jnp.where(half == 0, low, WIN_BLOCKS - 1 - low)
    shift = BASE_ROW - window * WIN_ROWS
    first = BASE_ROW + block * BLK
    query_row = first + (lax.broadcasted_iota(jnp.int32, (1, ROWS), 1) & (BLK - 1))
    query_from = jnp.zeros((1, ROWS), jnp.int32)
    begin = 0
    for entry in range(24):
        at = starts[entry] + shift
        query_from = jnp.where(query_row >= at, at, query_from)
        begin = jnp.where(first >= at, at, begin)
    end = first + BLK
    steps = (end - begin + TILE - 1) // TILE
    q, do = qd[0], qd[1]
    lse, delta = ld[pl.ds(2 * half, 1), :], ld[pl.ds(2 * half + 1, 1), :]
    dq_t[...] = jnp.zeros_like(dq_t)

    @pl.loop(0, steps)
    def _(step):
        row = pl.multiple_of(end - (step + 1) * TILE, BLK)
        rows = pl.ds(row, TILE)
        k, v = kv[0, rows, :], kv[1, rows, :]
        s = lax.dot_general(k, q, (((1,), (1,)), ((), ())), preferred_element_type=jnp.float32)
        dp = lax.dot_general(v, do, (((1,), (1,)), ((), ())), preferred_element_type=jnp.float32)
        key_row = row + lax.broadcasted_iota(jnp.int32, (TILE, 1), 0)
        allowed = (key_row <= query_row) & (key_row >= query_from)
        p = jnp.where(allowed, jnp.exp2(s * (SCALE * LOG2E) - lse), 0.0)
        ds = (p * (dp - delta)).astype(jnp.bfloat16)
        totals[1, rows, :] += jnp.dot(p.astype(jnp.bfloat16), do, preferred_element_type=jnp.float32)
        totals[0, rows, :] += jnp.dot(ds, q, preferred_element_type=jnp.float32)
        dq_t[...] += lax.dot_general(k, ds, (((0,), (0,)), ((), ())), preferred_element_type=jnp.float32)

    dq[...] = (dq_t[...].T * SCALE).astype(jnp.bfloat16)

    @pl.when((src == XS - 1) & (half == 1))
    def _():
        parts[0] = (totals[0] * SCALE).astype(jnp.bfloat16)
        parts[1] = totals[1].astype(jnp.bfloat16)


def grads(info, starts, qd, ld, kv):
    return pl.pallas_call(
        grads_kernel,
        grid_spec=pltpu.PrefetchScalarGridSpec(
            num_scalar_prefetch=2,
            grid=(XS, 2),
            in_specs=[
                pl.BlockSpec((None, 2, None, ROWS, DIM), lambda s, h, *_: (s, 0, h, 0, 0)),
                pl.BlockSpec((None, 8, ROWS), lambda s, h, *_: (s, 0, 0)),
                pl.BlockSpec(memory_space=pl.ANY),
            ],
            out_specs=[
                pl.BlockSpec((None, None, ROWS, DIM), lambda s, h, *_: (s, h, 0, 0)),
                pl.BlockSpec((2, KEY_ROWS, DIM), lambda s, h, *_: (0, 0, 0)),
            ],
            scratch_shapes=[
                pltpu.VMEM((2, KEY_ROWS, DIM), jnp.bfloat16),
                pltpu.VMEM((2, KEY_ROWS, DIM), jnp.float32),
                pltpu.VMEM((DIM, ROWS), jnp.float32),
                pltpu.SemaphoreType.DMA,
            ],
        ),
        out_shape=(
            jax.ShapeDtypeStruct((XS, 2, ROWS, DIM), jnp.bfloat16),
            jax.ShapeDtypeStruct((2, KEY_ROWS, DIM), jnp.bfloat16),
        ),
        compiler_params=pltpu.CompilerParams(
            dimension_semantics=("arbitrary", "arbitrary"), vmem_limit_bytes=40 * 2**20
        ),
        name="grads",
    )(info, starts, qd, ld, kv)


def collect_kernel(
    dq_src, parts, dq, dkv, own, sib, stage, near, far, final,
    dq_send, dq_recv, own_sem, core_send, core_recv, z_send, z_recv, next_send, next_recv,
    out_send, out_recv, last_sem,
):
    window, z, x, core = place()
    greet(window, z, x, core)

    def core_copy(gid):
        return remote(
            group_of(parts, gid, 1 - core), sib.at[gid],
            core_send.at[gid], core_recv.at[gid], device(window, z, x, 1 - core),
        )

    def own_copy(gid):
        return pltpu.make_async_copy(group_of(parts, gid, core), own.at[gid], own_sem.at[gid])

    def dq_copy(step):
        to = (x + step) % XS
        return remote(
            dq_src.at[to], dq.at[x], dq_send.at[step - 1], dq_recv.at[step - 1], device(window, z, to, core)
        )

    def dq_arrival(step):
        came = (x - step + XS) % XS
        return remote(
            dq_src.at[came], dq.at[came], dq_send.at[step - 1], dq_recv.at[step - 1],
            device(window, z, came, core),
        )

    dq_own = pltpu.make_async_copy(dq_src.at[x], dq.at[x], last_sem.at[0])

    def z_copy(gid, at):
        return remote(
            stage.at[gid], near.at[gid // 4, at], z_send.at[gid], z_recv.at[gid // 4, at],
            device(window, owner_z(gid), x, core),
        )

    def z_arrival(half, came):
        return remote(
            stage.at[0], near.at[half, came], z_send.at[0], z_recv.at[half, came],
            device(window, came, x, core),
        )

    def next_copy(gid, at):
        return remote(
            stage.at[gid], far.at[at], next_send.at[gid - 8], next_recv.at[at],
            device(window - 1, owner_z(gid), x, core),
        )

    def next_arrival(came):
        return remote(
            stage.at[0], far.at[came], next_send.at[0], next_recv.at[came],
            device(window, z, x, 1 - core),
        )

    def both(gid):
        return own[gid].astype(jnp.float32) + sib[gid].astype(jnp.float32)

    def level(at):
        mine = (at, at + 4)
        others = [gid for gid in reversed(NEED[at]) if gid < 8 and gid not in mine]
        previous = [gid for gid in NEED[at] if gid >= 8]
        order = (*others, *mine)

        if previous:

            @pl.when(window > 0)
            def _():
                for gid in previous:
                    core_copy(gid).start()
                    own_copy(gid).start()

        for gid in order:
            core_copy(gid).start()
            own_copy(gid).start()
        dq_own.start()
        for step in (2, 1, 3):
            dq_copy(step).start()

        if previous:

            @pl.when(window > 0)
            def _():
                for gid in previous:
                    own_copy(gid).wait()
                    core_copy(gid).wait_recv()
                    stage[gid] = both(gid).astype(jnp.bfloat16)
                    next_copy(gid, at).start()

        for gid in others:
            own_copy(gid).wait()
            core_copy(gid).wait_recv()
            stage[gid] = both(gid).astype(jnp.bfloat16)
            z_copy(gid, at).start()
        for gid in mine:
            half = gid // 4
            own_copy(gid).wait()
            core_copy(gid).wait_recv()
            total = both(gid)
            for came in range(ZS):
                if came != at and gid in NEED[came]:
                    z_arrival(half, came).wait_recv()
                    total = total + near[half, came].astype(jnp.float32)
            if half == 0 or at not in PRIOR_FROM:
                final[half] = total.astype(jnp.bfloat16)
            else:

                @pl.when(window < WINDOWS - 1)
                def _():
                    more = total
                    for came in PRIOR_TO:
                        next_arrival(came).wait_recv()
                        more = more + far[came].astype(jnp.float32)
                    final[half] = more.astype(jnp.bfloat16)

                @pl.when(window == WINDOWS - 1)
                def _():
                    final[half] = total.astype(jnp.bfloat16)

        for gid in order:
            core_copy(gid).wait_send()
        for gid in others:
            z_copy(gid, at).wait_send()
        if previous:

            @pl.when(window > 0)
            def _():
                for gid in previous:
                    core_copy(gid).wait_send()
                    next_copy(gid, at).wait_send()

    for at in range(ZS):
        pl.when(z == at)(lambda at=at: level(at))

    def piece(half, to):
        return final.at[half, :, to if half == 0 else 3 - to]

    def out_copy(step, half):
        to = (x + step) % XS
        return remote(
            piece(half, to), dkv.at[x, :, half],
            out_send.at[step - 1, half], out_recv.at[step - 1, half], device(window, z, to, core),
        )

    def out_arrival(step, half):
        came = (x - step + XS) % XS
        return remote(
            piece(half, came), dkv.at[came, :, half],
            out_send.at[step - 1, half], out_recv.at[step - 1, half], device(window, z, came, core),
        )

    for step in (2, 1, 3):
        for half in (0, 1):
            out_copy(step, half).start()
    out_own = [
        pltpu.make_async_copy(piece(half, x), dkv.at[x, :, half], last_sem.at[1 + half]) for half in (0, 1)
    ]
    for copy in out_own:
        copy.start()
    dq_own.wait()
    for copy in out_own:
        copy.wait()
    for step in (1, 2, 3):
        dq_arrival(step).wait_recv()
        dq_copy(step).wait_send()
        for half in (0, 1):
            out_arrival(step, half).wait_recv()
            out_copy(step, half).wait_send()


def collect(dq_src, parts):
    dma = pltpu.SemaphoreType.DMA
    anywhere = pl.BlockSpec(memory_space=pl.ANY)
    piece = (2, 4, BLK, DIM)
    return pl.pallas_call(
        collect_kernel,
        out_shape=(
            jax.ShapeDtypeStruct(dq_src.shape, jnp.bfloat16),
            jax.ShapeDtypeStruct((XS, 2, 2, BLK, DIM), jnp.bfloat16),
        ),
        in_specs=[anywhere] * 2,
        out_specs=[anywhere] * 2,
        scratch_shapes=[
            pltpu.VMEM((11, *piece), jnp.bfloat16),
            pltpu.VMEM((11, *piece), jnp.bfloat16),
            pltpu.VMEM((11, *piece), jnp.bfloat16),
            pltpu.VMEM((2, ZS, *piece), jnp.bfloat16),
            pltpu.VMEM((2, *piece), jnp.bfloat16),
            pltpu.VMEM((2, *piece), jnp.bfloat16),
            dma((3,)), dma((3,)), dma((11,)), dma((11,)), dma((11,)), dma((8,)), dma((2, ZS)),
            dma((3,)), dma((2,)), dma((3, 2)), dma((3, 2)), dma((3,)),
        ],
        compiler_params=pltpu.CompilerParams(
            collective_id=1, has_side_effects=True, vmem_limit_bytes=32 * 2**20
        ),
        name="collect",
    )(dq_src, parts)


def by_head(rows):
    cut = rows.reshape(2, BLK, KV, GROUP, DIM).transpose(2, 0, 3, 1, 4)
    return cut.reshape(KV, 2, ROWS, DIM)


def lanes(rows):
    return rows.reshape(KV, GROUP, 2, BLK).transpose(0, 2, 1, 3).reshape(KV, 2, ROWS)


def on_device(query, key, value, output, grad_output, lse, doc_starts):
    window, z, _, core = place()
    delta = jnp.einsum("qhd,qhd->hq", grad_output, output, preferred_element_type=jnp.float32)
    rows = jnp.stack([lanes(lse * LOG2E), lanes(delta)], axis=2).reshape(KV, 4, ROWS)
    ld_src = jnp.concatenate([rows, jnp.zeros_like(rows)], axis=1)
    qd_src = jnp.stack([by_head(query), by_head(grad_output)], axis=1)
    kv_src = jnp.stack([key, value]).reshape(2, 2, BLK, KV, DIM).transpose(3, 0, 1, 2, 4)
    kv, qd, ld = spread(kv_src, qd_src, ld_src)
    info = jnp.stack([window, z, core]).astype(jnp.int32)
    dq, parts = grads(info, doc_starts, qd, ld, kv.reshape(2, KEY_ROWS, DIM))
    dq_back, dkv = collect(dq, parts.reshape(2, PAIRS, 2, BLK, DIM))
    grad_query = (
        dq_back.reshape(KV, 2, GROUP, BLK, DIM).transpose(1, 3, 0, 2, 4).reshape(2 * BLK, KV * GROUP, DIM)
    )
    back = dkv.transpose(1, 2, 3, 0, 4).reshape(2, 2 * BLK, KV, DIM)
    return grad_query, back[0], back[1]


def solution(mesh):
    tokens = P(("outer", "inner"), None, None)
    return jax.shard_map(
        on_device,
        mesh=mesh,
        in_specs=(tokens, tokens, tokens, tokens, tokens, P(None, ("outer", "inner")), P()),
        out_specs=(tokens, tokens, tokens),
        check_vma=False,
    )
```

```python
import math

import jax
import jax.numpy as jnp
from jax import lax
from jax.experimental import pallas as pl
from jax.experimental.pallas import tpu as pltpu
from jax.sharding import PartitionSpec as P

MESH = pl.DeviceIdType.MESH
ZS, XS = 4, 4
KV, GROUP, DIM, BLK = 4, 6, 128, 64
ROWS = GROUP * BLK
WINDOWS = 8
WIN_BLOCKS = 64
WIN_ROWS = WIN_BLOCKS * BLK
PAD_PAIRS, PRIOR_PAIRS = 2, 12
BASE_PAIRS = PAD_PAIRS + PRIOR_PAIRS
PAIRS = BASE_PAIRS + WIN_BLOCKS // 2
KEY_ROWS = PAIRS * 2 * BLK
BASE_ROW = BASE_PAIRS * 2 * BLK
TILE = 256
SCALE = 1.0 / math.sqrt(DIM)
LOG2E = math.log2(math.e)

NEED = {
    0: (0, 4, 5, 2, 6, 3, 7, 8, 9, 10),
    1: (1, 5, 0, 2, 6, 3, 7, 8, 9, 10),
    2: (2, 6, 1, 3, 7, 0),
    3: (3, 7, 2, 1, 0),
}
SPREAD_ORDER = {0: (10, 9, 8, 5, 6, 2, 7, 3), 1: (6, 0, 2, 7, 3, 10, 9, 8), 2: (7, 1, 3, 0), 3: (2, 1, 0)}
COLLECT_ORDER = {0: (7, 3, 6, 2, 5, 8, 9, 10), 1: (8, 9, 10, 7, 3, 6, 2, 0), 2: (0, 1, 7, 3), 3: (0, 1, 2)}
PRIOR_FROM = (0, 1, 2)


def owner_z(gid):
    return gid % 4


def place():
    inner = lax.axis_index("inner")
    return lax.axis_index("outer"), inner // (2 * XS), (inner // 2) % XS, inner % 2


def device(window, z, x, core):
    return {"outer": window, "inner": (z * XS + x) * 2 + core}


def piece_of(ref, gid, core, x):
    z = owner_z(gid)
    if gid < 4:
        return ref.at[:, BASE_PAIRS + 4 * z + x, core]
    if gid < 8:
        return ref.at[:, BASE_PAIRS + 31 - 4 * z - x, 1 - core]
    return ref.at[:, PAD_PAIRS + 11 - 4 * z - x, 1 - core]


def block_of(ref, half, z, x, core):
    if half == 0:
        return ref.at[:, BASE_PAIRS + 4 * z + x, core]
    return ref.at[:, BASE_PAIRS + 31 - 4 * z - x, 1 - core]


def turn(x, step):
    return (x + step + XS) % XS


def has_next(window, z):
    return (window < WINDOWS - 1) & (z <= 2)


def has_previous(window, z):
    return (window > 0) & (z == 0)


def greet(window, z, x, core):
    barrier = pltpu.get_barrier_semaphore()

    def signal(*where):
        pl.semaphore_signal(barrier, inc=1, device_id=device(*where), device_id_type=MESH)

    for step in range(1, XS):
        signal(window, z, (x + step) % XS, core)
    signal(window, z, x, 1 - core)
    pl.when(z > 0)(lambda: signal(window, z - 1, x, core))
    pl.when(z < ZS - 1)(lambda: signal(window, z + 1, x, core))
    pl.when(has_next(window, z))(lambda: signal(window + 1, 0, x, core))

    @pl.when(has_previous(window, z))
    def _():
        for other in PRIOR_FROM:
            signal(window - 1, other, x, core)

    count = 4 + jnp.where(z > 0, 1, 0) + jnp.where(z < ZS - 1, 1, 0)
    count = count + jnp.where(has_next(window, z), 1, 0) + jnp.where(has_previous(window, z), 3, 0)
    pl.semaphore_wait(barrier, count)


def remote(src, dst, send, recv, where):
    return pltpu.make_async_remote_copy(
        src_ref=src, dst_ref=dst, send_sem=send, recv_sem=recv, device_id=where, device_id_type=MESH
    )


def spread_kernel(
    kv_src, qd_src, ld_src, kv, qd, ld,
    kv_send, kv_recv, qd_send, qd_recv, ld_send, ld_recv,
    z_send, z_recv, next_send, next_recv, core_send, core_recv, own_sem,
):
    window, z, x, core = place()
    greet(window, z, x, core)

    def kv_copy(step, half):
        to = turn(x, step)
        return remote(
            kv_src.at[to, :, half], block_of(kv, half, z, x, core),
            kv_send.at[step, half], kv_recv.at[step, half], device(window, z, to, core),
        )

    def kv_arrival(step, half):
        came = turn(x, -step)
        return remote(
            kv_src.at[came, :, half], block_of(kv, half, z, came, core),
            kv_send.at[step, half], kv_recv.at[step, half], device(window, z, came, core),
        )

    def wide(src, dst, send, recv, step):
        to = turn(x, step)
        return remote(
            src.at[to], dst.at[step - 1], send.at[step - 1], recv.at[step - 1], device(window, z, to, core)
        )

    for step in (2, 1, 3):
        for half in (1, 0):
            kv_copy(step, half).start()
    own = [
        pltpu.make_async_copy(kv_src.at[x, :, half], block_of(kv, half, z, x, core), own_sem.at[half])
        for half in (0, 1)
    ]

    def z_copy(gid, j, at, way, src=None):
        piece = piece_of(kv, gid, core, turn(x, -j))
        return remote(
            piece if src is None else src, piece,
            z_send.at[gid, (way + 1) // 2, j], z_recv.at[gid, j], device(window, at + way, x, core),
        )

    def next_copy(gid, j, src=None):
        piece = piece_of(kv, gid, core, turn(x, -j))
        return remote(
            piece if src is None else src, piece_of(kv, gid + 4, core, turn(x, -j)),
            next_send.at[j], next_recv.at[gid - 4, j], device(window + 1, 0, x, core),
        )

    def next_arrival(gid, j):
        piece = piece_of(kv, gid, core, turn(x, -j))
        return remote(piece, piece, next_send.at[j], next_recv.at[gid - 8, j], device(window, z, x, 1 - core))

    def core_copy(gid, j, src=None):
        piece = piece_of(kv, gid, core, turn(x, -j))
        return remote(
            piece if src is None else src, piece,
            core_send.at[gid, j], core_recv.at[gid, j], device(window, z, x, 1 - core),
        )

    def core_arrival(gid, j):
        piece = piece_of(kv, gid, 1 - core, turn(x, -j))
        return remote(piece, piece, core_send.at[gid, j], core_recv.at[gid, j], device(window, z, x, 1 - core))

    def level(at):
        def ways(gid):
            owner = 0 if gid >= 8 else owner_z(gid)
            return [
                way
                for way in (-1, 1)
                if 0 <= at + way < ZS and gid in NEED[at + way] and abs(at + way - owner) > abs(at - owner)
            ]

        def onward(gid, j, src=None):
            for way in ways(gid):
                z_copy(gid, j, at, way, src).start()
            core_copy(gid, j, src).start()

        def guarded(gid, act):
            if gid >= 8:
                pl.when(window > 0)(act)
            else:
                act()

        def given(j, src=False):
            for gid in (at + 4, at):
                first = kv_src.at[x, :, gid // 4] if src else None
                if gid >= 4 and at in PRIOR_FROM:
                    pl.when(window < WINDOWS - 1)(lambda: next_copy(gid, j, first).start())
                onward(gid, j, first)

        def arrived(gid, j):
            if gid >= 8 and at == 0:
                next_arrival(gid, j).wait_recv()
            else:
                z_copy(gid, j, at, 1 if at < ZS - 1 else -1).wait_recv()
            onward(gid, j)

        given(0, True)
        for copy in own:
            copy.start()
        for step in (2, 1, 3):
            wide(ld_src, ld, ld_send, ld_recv, step).start()
            wide(qd_src, qd, qd_send, qd_recv, step).start()

        @pl.loop(1, XS)
        def _(j):
            for half in (0, 1):
                kv_arrival(j, half).wait_recv()
            given(j)

        for gid in SPREAD_ORDER[at]:
            guarded(gid, lambda: pl.loop(0, XS)(lambda j: arrived(gid, j)))

        @pl.loop(0, XS)
        def _(j):
            for gid in NEED[at]:

                def act():
                    core_arrival(gid, j).wait_recv()
                    core_copy(gid, j).wait_send()
                    for way in ways(gid):
                        z_copy(gid, j, at, way).wait_send()

                guarded(gid, act)
            if at in PRIOR_FROM:
                pl.when(window < WINDOWS - 1)(lambda: next_copy(at + 4, j).wait_send())

    for at in range(ZS):
        pl.when(z == at)(lambda at=at: level(at))

    for copy in own:
        copy.wait()
    for step in (1, 2, 3):
        for half in (0, 1):
            kv_copy(step, half).wait_send()
        wide(ld_src, ld, ld_send, ld_recv, step).wait()
        wide(qd_src, qd, qd_send, qd_recv, step).wait()


def spread(kv_src, qd_src, ld_src):
    dma = pltpu.SemaphoreType.DMA
    anywhere = pl.BlockSpec(memory_space=pl.ANY)
    return pl.pallas_call(
        spread_kernel,
        out_shape=(
            jax.ShapeDtypeStruct((2, PAIRS, 2, BLK, DIM), jnp.bfloat16),
            jax.ShapeDtypeStruct((XS - 1, *qd_src.shape[1:]), jnp.bfloat16),
            jax.ShapeDtypeStruct((XS - 1, *ld_src.shape[1:]), jnp.float32),
        ),
        in_specs=[anywhere] * 3,
        out_specs=[anywhere] * 3,
        scratch_shapes=[
            dma((XS, 2)), dma((XS, 2)), dma((3,)), dma((3,)), dma((3,)), dma((3,)),
            dma((11, 2, XS)), dma((11, XS)), dma((XS,)), dma((3, XS)), dma((11, XS)), dma((11, XS)), dma((2,)),
        ],
        compiler_params=pltpu.CompilerParams(collective_id=0, has_side_effects=True),
        name="spread",
    )(kv_src, qd_src, ld_src)


def grads_kernel(info, starts, qd_own, ld_own, qd, ld, kv_hbm, dq, parts, kv, totals, dq_t, kv_sem):
    step, half = pl.program_id(0), pl.program_id(1)
    window, z, core = info[0], info[1], info[2]
    src = (info[3] - step + XS) % XS

    @pl.when((step == 0) & (half == 0))
    def _():
        load = pltpu.make_async_copy(kv_hbm, kv, kv_sem)
        load.start()
        totals[...] = jnp.zeros_like(totals)
        load.wait()

        def clear(first, blocks):
            kv[:, pl.ds(first * BLK, blocks * BLK), :] = jnp.zeros((2, blocks * BLK, DIM), jnp.bfloat16)

        clear(0, 2 * PAD_PAIRS)
        pl.when((z >= 2) | (window == 0))(lambda: clear(2 * PAD_PAIRS, 2 * PRIOR_PAIRS))
        pl.when(z == 0)(lambda: clear(2 * BASE_PAIRS + 8, 8))

    low = 8 * z + 2 * src + core
    block = jnp.where(half == 0, low, WIN_BLOCKS - 1 - low)
    shift = BASE_ROW - window * WIN_ROWS
    first = BASE_ROW + block * BLK
    query_row = first + (lax.broadcasted_iota(jnp.int32, (1, ROWS), 1) & (BLK - 1))
    query_from = jnp.zeros((1, ROWS), jnp.int32)
    begin = 0
    for entry in range(24):
        at = starts[entry] + shift
        query_from = jnp.where(query_row >= at, at, query_from)
        begin = jnp.where(first >= at, at, begin)
    end = first + BLK
    tiles = (end - begin + TILE - 1) // TILE
    q = jnp.where(step == 0, qd_own[0], qd[0])
    do = jnp.where(step == 0, qd_own[1], qd[1])
    row_at = pl.ds(2 * half, 1)
    lse = jnp.where(step == 0, ld_own[row_at, :], ld[row_at, :])
    row_at = pl.ds(2 * half + 1, 1)
    delta = jnp.where(step == 0, ld_own[row_at, :], ld[row_at, :])
    dq_t[...] = jnp.zeros_like(dq_t)

    @pl.loop(0, tiles)
    def _(tile):
        row = pl.multiple_of(end - (tile + 1) * TILE, BLK)
        rows = pl.ds(row, TILE)
        k, v = kv[0, rows, :], kv[1, rows, :]
        s = lax.dot_general(k, q, (((1,), (1,)), ((), ())), preferred_element_type=jnp.float32)
        dp = lax.dot_general(v, do, (((1,), (1,)), ((), ())), preferred_element_type=jnp.float32)
        key_row = row + lax.broadcasted_iota(jnp.int32, (TILE, 1), 0)
        allowed = (key_row <= query_row) & (key_row >= query_from)
        p = jnp.where(allowed, jnp.exp2(s * (SCALE * LOG2E) - lse), 0.0)
        ds = (p * (dp - delta)).astype(jnp.bfloat16)
        totals[1, rows, :] += jnp.dot(p.astype(jnp.bfloat16), do, preferred_element_type=jnp.float32)
        totals[0, rows, :] += jnp.dot(ds, q, preferred_element_type=jnp.float32)
        dq_t[...] += lax.dot_general(k, ds, (((0,), (0,)), ((), ())), preferred_element_type=jnp.float32)

    dq[...] = (dq_t[...].T * SCALE).astype(jnp.bfloat16)

    @pl.when((step == XS - 1) & (half == 1))
    def _():
        parts[0] = (totals[0] * SCALE).astype(jnp.bfloat16)
        parts[1] = totals[1].astype(jnp.bfloat16)


def grads(info, starts, qd_own, ld_own, qd, ld, kv):
    return pl.pallas_call(
        grads_kernel,
        grid_spec=pltpu.PrefetchScalarGridSpec(
            num_scalar_prefetch=2,
            grid=(XS, 2),
            in_specs=[
                pl.BlockSpec(
                    (None, 2, None, ROWS, DIM),
                    lambda s, h, info, _: (info[3], 0, jnp.where(s == 0, h, 1), 0, 0),
                ),
                pl.BlockSpec((None, 8, ROWS), lambda s, h, info, _: (info[3], 0, 0)),
                pl.BlockSpec(
                    (None, 2, None, ROWS, DIM),
                    lambda s, h, *_: (jnp.maximum(s - 1, 0), 0, jnp.where(s == 0, 0, h), 0, 0),
                ),
                pl.BlockSpec((None, 8, ROWS), lambda s, h, *_: (jnp.maximum(s - 1, 0), 0, 0)),
                pl.BlockSpec(memory_space=pl.ANY),
            ],
            out_specs=[
                pl.BlockSpec((None, None, ROWS, DIM), lambda s, h, *_: (s, h, 0, 0)),
                pl.BlockSpec((2, KEY_ROWS, DIM), lambda s, h, *_: (0, 0, 0)),
            ],
            scratch_shapes=[
                pltpu.VMEM((2, KEY_ROWS, DIM), jnp.bfloat16),
                pltpu.VMEM((2, KEY_ROWS, DIM), jnp.float32),
                pltpu.VMEM((DIM, ROWS), jnp.float32),
                pltpu.SemaphoreType.DMA,
            ],
        ),
        out_shape=(
            jax.ShapeDtypeStruct((XS, 2, ROWS, DIM), jnp.bfloat16),
            jax.ShapeDtypeStruct((2, KEY_ROWS, DIM), jnp.bfloat16),
        ),
        compiler_params=pltpu.CompilerParams(
            dimension_semantics=("arbitrary", "arbitrary"), vmem_limit_bytes=40 * 2**20
        ),
        name="grads",
    )(info, starts, qd_own, ld_own, qd, ld, kv)


def collect_kernel(
    dq_src, parts, dq, dkv, own, sib, stage, near, far, final,
    dq_send, dq_recv, own_sem, core_send, core_recv, z_send, z_recv, next_send, next_recv,
    out_send, out_recv, last_sem,
):
    window, z, x, core = place()
    greet(window, z, x, core)

    def core_copy(gid, j):
        return remote(
            piece_of(parts, gid, 1 - core, turn(x, j + 1)), sib.at[gid, j],
            core_send.at[gid, j], core_recv.at[gid, j], device(window, z, x, 1 - core),
        )

    def own_copy(gid, j):
        return pltpu.make_async_copy(piece_of(parts, gid, core, turn(x, j + 1)), own.at[gid, j], own_sem.at[gid, j])

    def dq_copy(step):
        to = turn(x, -step)
        return remote(
            dq_src.at[step], dq.at[x], dq_send.at[step - 1], dq_recv.at[step - 1], device(window, z, to, core)
        )

    def dq_arrival(step):
        came = turn(x, step)
        return remote(
            dq_src.at[step], dq.at[came], dq_send.at[step - 1], dq_recv.at[step - 1],
            device(window, z, came, core),
        )

    def out_copy(half, j):
        return remote(
            final.at[half, j], dkv.at[x, :, half],
            out_send.at[half, j], out_recv.at[half, j], device(window, z, turn(x, j + 1), core),
        )

    def out_arrival(half, j):
        came = turn(x, -j - 1)
        return remote(
            final.at[half, j], dkv.at[came, :, half],
            out_send.at[half, j], out_recv.at[half, j], device(window, z, came, core),
        )

    def out_own(half):
        return pltpu.make_async_copy(final.at[half, XS - 1], dkv.at[x, :, half], last_sem.at[1 + half])

    dq_own = pltpu.make_async_copy(dq_src.at[0], dq.at[x], last_sem.at[0])

    def z_copy(gid, j, at, way):
        return remote(
            stage.at[gid, j], near.at[gid, (1 - way) // 2, j],
            z_send.at[gid, j], z_recv.at[gid, (1 - way) // 2, j], device(window, at + way, x, core),
        )

    def next_copy(gid, j):
        return remote(
            stage.at[gid, j], far.at[j], next_send.at[gid - 8, j], next_recv.at[j],
            device(window - 1, owner_z(gid), x, core),
        )

    def next_arrival(j):
        return remote(
            stage.at[8, j], far.at[j], next_send.at[0, j], next_recv.at[j], device(window, z, x, 1 - core),
        )

    def level(at):
        order = COLLECT_ORDER[at]
        mine = (at, at + 4)

        def each(gids, act, j):
            for gid in gids:
                if gid >= 8:
                    pl.when(window > 0)(lambda: act(gid, j))
                else:
                    act(gid, j)

        def begin(gid, j):
            core_copy(gid, j).start()
            own_copy(gid, j).start()

        def towards(gid):
            owner = 0 if gid >= 8 else owner_z(gid)
            return 1 if owner > at else -1

        def summed(gid, j):
            own_copy(gid, j).wait()
            core_copy(gid, j).wait_recv()
            total = own[gid, j].astype(jnp.float32) + sib[gid, j].astype(jnp.float32)
            owner = 0 if gid >= 8 else owner_z(gid)
            for way in (-1, 1):
                came = at + way
                if 0 <= came < ZS and gid in NEED[came] and abs(came - owner) > abs(at - owner):
                    z_copy(gid, j, came, -way).wait_recv()
                    total = total + near[gid, (way + 1) // 2, j].astype(jnp.float32)
            return total

        def pass_on(gid, j):
            stage[gid, j] = summed(gid, j).astype(jnp.bfloat16)
            if gid >= 8 and at == 0:
                next_copy(gid, j).start()
            else:
                z_copy(gid, j, at, towards(gid)).start()

        def keep(half, j):
            total = summed(mine[half], j)
            if half == 0 or at not in PRIOR_FROM:
                final[half, j] = total.astype(jnp.bfloat16)
            else:

                @pl.when(window < WINDOWS - 1)
                def _():
                    next_arrival(j).wait_recv()
                    final[half, j] = (total + far[j].astype(jnp.float32)).astype(jnp.bfloat16)

                @pl.when(window == WINDOWS - 1)
                def _():
                    final[half, j] = total.astype(jnp.bfloat16)

        def finish(gid, j):
            core_copy(gid, j).wait_send()
            if gid in mine:
                return
            if gid >= 8 and at == 0:
                next_copy(gid, j).wait_send()
            else:
                z_copy(gid, j, at, towards(gid)).wait_send()

        @pl.loop(0, XS)
        def _(j):
            each((*order, *mine), begin, j)

        dq_own.start()
        for step in (2, 1, 3):
            dq_copy(step).start()
        for gid in order:
            each([gid], lambda gid, _: pl.loop(0, XS)(lambda j: pass_on(gid, j)), None)
        for half in (0, 1):

            @pl.loop(0, XS - 1)
            def _(j):
                keep(half, j)
                out_copy(half, j).start()

            keep(half, XS - 1)
            out_own(half).start()

        @pl.loop(0, XS)
        def _(j):
            each((*order, *mine), finish, j)

    for at in range(ZS):
        pl.when(z == at)(lambda at=at: level(at))

    dq_own.wait()
    for half in (0, 1):
        out_own(half).wait()
    for step in (1, 2, 3):
        dq_arrival(step).wait_recv()
        dq_copy(step).wait_send()
        for half in (0, 1):
            out_arrival(half, step - 1).wait_recv()
            out_copy(half, step - 1).wait_send()


def collect(dq_src, parts):
    dma = pltpu.SemaphoreType.DMA
    anywhere = pl.BlockSpec(memory_space=pl.ANY)
    piece = (2, BLK, DIM)
    return pl.pallas_call(
        collect_kernel,
        out_shape=(
            jax.ShapeDtypeStruct(dq_src.shape, jnp.bfloat16),
            jax.ShapeDtypeStruct((XS, 2, 2, BLK, DIM), jnp.bfloat16),
        ),
        in_specs=[anywhere] * 2,
        out_specs=[anywhere] * 2,
        scratch_shapes=[
            pltpu.VMEM((11, XS, *piece), jnp.bfloat16),
            pltpu.VMEM((11, XS, *piece), jnp.bfloat16),
            pltpu.VMEM((11, XS, *piece), jnp.bfloat16),
            pltpu.VMEM((11, 2, XS, *piece), jnp.bfloat16),
            pltpu.VMEM((XS, *piece), jnp.bfloat16),
            pltpu.VMEM((2, XS, *piece), jnp.bfloat16),
            dma((3,)), dma((3,)), dma((11, XS)), dma((11, XS)), dma((11, XS)), dma((11, XS)), dma((11, 2, XS)),
            dma((3, XS)), dma((XS,)), dma((2, XS)), dma((2, XS)), dma((3,)),
        ],
        compiler_params=pltpu.CompilerParams(
            collective_id=1, has_side_effects=True, vmem_limit_bytes=32 * 2**20
        ),
        name="collect",
    )(dq_src, parts)


def by_head(rows):
    cut = rows.reshape(2, BLK, KV, GROUP, DIM).transpose(2, 0, 3, 1, 4)
    return cut.reshape(KV, 2, ROWS, DIM)


def lanes(rows):
    return rows.reshape(KV, GROUP, 2, BLK).transpose(0, 2, 1, 3).reshape(KV, 2, ROWS)


def on_device(query, key, value, output, grad_output, lse, doc_starts):
    window, z, x, core = place()
    delta = jnp.einsum("qhd,qhd->hq", grad_output, output, preferred_element_type=jnp.float32)
    rows = jnp.stack([lanes(lse * LOG2E), lanes(delta)], axis=2).reshape(KV, 4, ROWS)
    ld_src = jnp.concatenate([rows, jnp.zeros_like(rows)], axis=1)
    qd_src = jnp.stack([by_head(query), by_head(grad_output)], axis=1)
    kv_src = jnp.stack([key, value]).reshape(2, 2, BLK, KV, DIM).transpose(3, 0, 1, 2, 4)
    kv, qd, ld = spread(kv_src, qd_src, ld_src)
    info = jnp.stack([window, z, core, x]).astype(jnp.int32)
    dq, parts = grads(info, doc_starts, qd_src, ld_src, qd, ld, kv.reshape(2, KEY_ROWS, DIM))
    dq_back, dkv = collect(dq, parts.reshape(2, PAIRS, 2, BLK, DIM))
    grad_query = (
        dq_back.reshape(KV, 2, GROUP, BLK, DIM).transpose(1, 3, 0, 2, 4).reshape(2 * BLK, KV * GROUP, DIM)
    )
    back = dkv.transpose(1, 2, 3, 0, 4).reshape(2, 2 * BLK, KV, DIM)
    return grad_query, back[0], back[1]


def solution(mesh):
    tokens = P(("outer", "inner"), None, None)
    return jax.shard_map(
        on_device,
        mesh=mesh,
        in_specs=(tokens, tokens, tokens, tokens, tokens, P(None, ("outer", "inner")), P()),
        out_specs=(tokens, tokens, tokens),
        check_vma=False,
    )
```

```python
import math

import jax
import jax.numpy as jnp
from jax import lax
from jax.experimental import pallas as pl
from jax.experimental.pallas import tpu as pltpu
from jax.sharding import PartitionSpec as P

MESH = pl.DeviceIdType.MESH
ZS, XS = 4, 4
KV, GROUP, DIM, BLK = 4, 6, 128, 64
ROWS = GROUP * BLK
WINDOWS = 8
WIN_BLOCKS = 64
WIN_ROWS = WIN_BLOCKS * BLK
PAD_PAIRS, PRIOR_PAIRS = 2, 12
BASE_PAIRS = PAD_PAIRS + PRIOR_PAIRS
PAIRS = BASE_PAIRS + WIN_BLOCKS // 2
KEY_ROWS = PAIRS * 2 * BLK
BASE_ROW = BASE_PAIRS * 2 * BLK
TILE = 256
SCALE = 1.0 / math.sqrt(DIM)
LOG2E = math.log2(math.e)

NEED = {
    0: (0, 4, 5, 2, 6, 3, 7, 8, 9, 10),
    1: (1, 5, 0, 2, 6, 3, 7, 8, 9, 10),
    2: (2, 6, 1, 3, 7, 0),
    3: (3, 7, 2, 1, 0),
}
SPREAD_ORDER = {0: (10, 9, 8, 5, 6, 2, 7, 3), 1: (6, 0, 2, 7, 3, 10, 9, 8), 2: (7, 1, 3, 0), 3: (2, 1, 0)}
COLLECT_ORDER = {0: (7, 3, 6, 2, 5, 8, 9, 10), 1: (8, 9, 10, 7, 3, 6, 2, 0), 2: (0, 1, 7, 3), 3: (0, 1, 2)}
PRIOR_FROM = (0, 1, 2)


def owner_z(gid):
    return gid % 4


def place():
    inner = lax.axis_index("inner")
    return lax.axis_index("outer"), inner // (2 * XS), (inner // 2) % XS, inner % 2


def device(window, z, x, core):
    return {"outer": window, "inner": (z * XS + x) * 2 + core}


def piece_of(ref, gid, core, x):
    z = owner_z(gid)
    if gid < 4:
        return ref.at[:, BASE_PAIRS + 4 * z + x, core]
    if gid < 8:
        return ref.at[:, BASE_PAIRS + 31 - 4 * z - x, 1 - core]
    return ref.at[:, PAD_PAIRS + 11 - 4 * z - x, 1 - core]


def block_of(ref, half, z, x, core):
    if half == 0:
        return ref.at[:, BASE_PAIRS + 4 * z + x, core]
    return ref.at[:, BASE_PAIRS + 31 - 4 * z - x, 1 - core]


def turn(x, step):
    return (x + step + XS) % XS


def has_next(window, z):
    return (window < WINDOWS - 1) & (z <= 2)


def has_previous(window, z):
    return (window > 0) & (z == 0)


def greet(window, z, x, core):
    barrier = pltpu.get_barrier_semaphore()

    def signal(*where):
        pl.semaphore_signal(barrier, inc=1, device_id=device(*where), device_id_type=MESH)

    for step in range(1, XS):
        signal(window, z, (x + step) % XS, core)
    signal(window, z, x, 1 - core)
    pl.when(z > 0)(lambda: signal(window, z - 1, x, core))
    pl.when(z < ZS - 1)(lambda: signal(window, z + 1, x, core))
    pl.when(has_next(window, z))(lambda: signal(window + 1, 0, x, core))

    @pl.when(has_previous(window, z))
    def _():
        for other in PRIOR_FROM:
            signal(window - 1, other, x, core)

    count = 4 + jnp.where(z > 0, 1, 0) + jnp.where(z < ZS - 1, 1, 0)
    count = count + jnp.where(has_next(window, z), 1, 0) + jnp.where(has_previous(window, z), 3, 0)
    pl.semaphore_wait(barrier, count)


def remote(src, dst, send, recv, where):
    return pltpu.make_async_remote_copy(
        src_ref=src, dst_ref=dst, send_sem=send, recv_sem=recv, device_id=where, device_id_type=MESH
    )


def spread_kernel(
    kv_src, qd_src, ld_src, kv, qd, ld,
    kv_send, kv_recv, qd_send, qd_recv, ld_send, ld_recv,
    z_send, z_recv, next_send, next_recv, core_send, core_recv, own_sem,
):
    window, z, x, core = place()
    greet(window, z, x, core)

    def kv_copy(step, half):
        to = turn(x, step)
        return remote(
            kv_src.at[to, :, half], block_of(kv, half, z, x, core),
            kv_send.at[step, half], kv_recv.at[step, half], device(window, z, to, core),
        )

    def kv_arrival(step, half):
        came = turn(x, -step)
        return remote(
            kv_src.at[came, :, half], block_of(kv, half, z, came, core),
            kv_send.at[step, half], kv_recv.at[step, half], device(window, z, came, core),
        )

    def wide(src, dst, send, recv, step):
        to = turn(x, step)
        return remote(
            src.at[to], dst.at[step - 1], send.at[step - 1], recv.at[step - 1], device(window, z, to, core)
        )

    for step in (2, 1, 3):
        for half in (1, 0):
            kv_copy(step, half).start()
    own = [
        pltpu.make_async_copy(kv_src.at[x, :, half], block_of(kv, half, z, x, core), own_sem.at[half])
        for half in (0, 1)
    ]

    def z_copy(gid, j, at, way, src=None):
        piece = piece_of(kv, gid, core, turn(x, -j))
        return remote(
            piece if src is None else src, piece,
            z_send.at[gid, (way + 1) // 2, j], z_recv.at[gid, j], device(window, at + way, x, core),
        )

    def next_copy(gid, j, src=None):
        piece = piece_of(kv, gid, core, turn(x, -j))
        return remote(
            piece if src is None else src, piece_of(kv, gid + 4, core, turn(x, -j)),
            next_send.at[j], next_recv.at[gid - 4, j], device(window + 1, 0, x, core),
        )

    def next_arrival(gid, j):
        piece = piece_of(kv, gid, core, turn(x, -j))
        return remote(piece, piece, next_send.at[j], next_recv.at[gid - 8, j], device(window, z, x, 1 - core))

    def core_copy(gid, j, src=None):
        piece = piece_of(kv, gid, core, turn(x, -j))
        return remote(
            piece if src is None else src, piece,
            core_send.at[gid, j], core_recv.at[gid, j], device(window, z, x, 1 - core),
        )

    def core_arrival(gid, j):
        piece = piece_of(kv, gid, 1 - core, turn(x, -j))
        return remote(piece, piece, core_send.at[gid, j], core_recv.at[gid, j], device(window, z, x, 1 - core))

    def level(at):
        def ways(gid):
            owner = 0 if gid >= 8 else owner_z(gid)
            return [
                way
                for way in (-1, 1)
                if 0 <= at + way < ZS and gid in NEED[at + way] and abs(at + way - owner) > abs(at - owner)
            ]

        def onward(gid, j, src=None):
            for way in ways(gid):
                z_copy(gid, j, at, way, src).start()
            core_copy(gid, j, src).start()

        def guarded(gid, act):
            if gid >= 8:
                pl.when(window > 0)(act)
            else:
                act()

        def given(j, src=False):
            for gid in (at + 4, at):
                first = kv_src.at[x, :, gid // 4] if src else None
                if gid >= 4 and at in PRIOR_FROM:
                    pl.when(window < WINDOWS - 1)(lambda: next_copy(gid, j, first).start())
                onward(gid, j, first)

        def arrived(gid, j):
            if gid >= 8 and at == 0:
                next_arrival(gid, j).wait_recv()
            else:
                z_copy(gid, j, at, 1 if at < ZS - 1 else -1).wait_recv()
            onward(gid, j)

        given(0, True)
        for copy in own:
            copy.start()
        for step in (2, 1, 3):
            wide(ld_src, ld, ld_send, ld_recv, step).start()
            wide(qd_src, qd, qd_send, qd_recv, step).start()

        @pl.loop(1, XS)
        def _(j):
            for half in (0, 1):
                kv_arrival(j, half).wait_recv()
            given(j)

        for gid in SPREAD_ORDER[at]:
            guarded(gid, lambda: pl.loop(0, XS)(lambda j: arrived(gid, j)))

        @pl.loop(0, XS)
        def _(j):
            for gid in NEED[at]:

                def act():
                    core_arrival(gid, j).wait_recv()
                    core_copy(gid, j).wait_send()
                    for way in ways(gid):
                        z_copy(gid, j, at, way).wait_send()

                guarded(gid, act)
            if at in PRIOR_FROM:
                pl.when(window < WINDOWS - 1)(lambda: next_copy(at + 4, j).wait_send())

    for at in range(ZS):
        pl.when(z == at)(lambda at=at: level(at))

    for copy in own:
        copy.wait()
    for step in (1, 2, 3):
        for half in (0, 1):
            kv_copy(step, half).wait_send()
        wide(ld_src, ld, ld_send, ld_recv, step).wait()
        wide(qd_src, qd, qd_send, qd_recv, step).wait()


def spread(kv_src, qd_src, ld_src):
    dma = pltpu.SemaphoreType.DMA
    anywhere = pl.BlockSpec(memory_space=pl.ANY)
    return pl.pallas_call(
        spread_kernel,
        out_shape=(
            jax.ShapeDtypeStruct((2, PAIRS, 2, BLK, DIM), jnp.bfloat16),
            jax.ShapeDtypeStruct((XS - 1, *qd_src.shape[1:]), jnp.bfloat16),
            jax.ShapeDtypeStruct((XS - 1, *ld_src.shape[1:]), jnp.float32),
        ),
        in_specs=[anywhere] * 3,
        out_specs=[anywhere] * 3,
        scratch_shapes=[
            dma((XS, 2)), dma((XS, 2)), dma((3,)), dma((3,)), dma((3,)), dma((3,)),
            dma((11, 2, XS)), dma((11, XS)), dma((XS,)), dma((3, XS)), dma((11, XS)), dma((11, XS)), dma((2,)),
        ],
        compiler_params=pltpu.CompilerParams(collective_id=0, has_side_effects=True),
        name="spread",
    )(kv_src, qd_src, ld_src)


def grads_kernel(info, starts, qd_own, ld_own, qd, ld, kv_hbm, dq, parts, kv, totals, dq_t, held, kv_sem):
    step, half = pl.program_id(0), pl.program_id(1)
    window, z, core = info[0], info[1], info[2]
    src = (info[3] - step + XS) % XS

    @pl.when((step == 0) & (half == 0))
    def _():
        load = pltpu.make_async_copy(kv_hbm, kv, kv_sem)
        load.start()
        totals[...] = jnp.zeros_like(totals)
        load.wait()

        def clear(first, blocks):
            kv[:, pl.ds(first * BLK, blocks * BLK), :] = jnp.zeros((2, blocks * BLK, DIM), jnp.bfloat16)

        clear(0, 2 * PAD_PAIRS)
        pl.when((z >= 2) | (window == 0))(lambda: clear(2 * PAD_PAIRS, 2 * PRIOR_PAIRS))
        pl.when(z == 0)(lambda: clear(2 * BASE_PAIRS + 8, 8))

    low = 8 * z + 2 * src + core
    block = jnp.where(half == 0, low, WIN_BLOCKS - 1 - low)
    shift = BASE_ROW - window * WIN_ROWS
    first = BASE_ROW + block * BLK
    query_row = first + (lax.broadcasted_iota(jnp.int32, (1, ROWS), 1) & (BLK - 1))
    query_from = jnp.zeros((1, ROWS), jnp.int32)
    begin = 0
    for entry in range(24):
        at = starts[entry] + shift
        query_from = jnp.where(query_row >= at, at, query_from)
        begin = jnp.where(first >= at, at, begin)
    end = first + BLK
    tiles = (end - begin + TILE - 1) // TILE
    q = jnp.where(step == 0, qd_own[0], qd[0])
    do = jnp.where(step == 0, qd_own[1], qd[1])
    row_at = pl.ds(2 * half, 1)
    lse = jnp.where(step == 0, ld_own[row_at, :], ld[row_at, :])
    row_at = pl.ds(2 * half + 1, 1)
    delta = jnp.where(step == 0, ld_own[row_at, :], ld[row_at, :])
    dq_t[...] = jnp.zeros_like(dq_t)

    def scores(tile):
        row = pl.multiple_of(end - (tile + 1) * TILE, BLK)
        rows = pl.ds(row, TILE)
        s = lax.dot_general(kv[0, rows, :], q, (((1,), (1,)), ((), ())), preferred_element_type=jnp.float32)
        dp = lax.dot_general(kv[1, rows, :], do, (((1,), (1,)), ((), ())), preferred_element_type=jnp.float32)
        key_row = row + lax.broadcasted_iota(jnp.int32, (TILE, 1), 0)
        allowed = (key_row <= query_row) & (key_row >= query_from)
        p = jnp.where(allowed, jnp.exp2(s * (SCALE * LOG2E) - lse), 0.0)
        return p.astype(jnp.bfloat16), (p * (dp - delta)).astype(jnp.bfloat16)

    def products(tile, p, ds):
        rows = pl.ds(pl.multiple_of(end - (tile + 1) * TILE, BLK), TILE)
        totals[1, rows, :] += jnp.dot(p, do, preferred_element_type=jnp.float32)
        totals[0, rows, :] += jnp.dot(ds, q, preferred_element_type=jnp.float32)
        dq_t[...] += lax.dot_general(kv[0, rows, :], ds, (((0,), (0,)), ((), ())), preferred_element_type=jnp.float32)

    held[0], held[1] = scores(0)

    @pl.loop(1, tiles)
    def _(tile):
        p, ds = held[0], held[1]
        new_p, new_ds = scores(tile)
        products(tile - 1, p, ds)
        held[0], held[1] = new_p, new_ds

    products(tiles - 1, held[0], held[1])

    dq[...] = (dq_t[...].T * SCALE).astype(jnp.bfloat16)

    @pl.when((step == XS - 1) & (half == 1))
    def _():
        parts[0] = (totals[0] * SCALE).astype(jnp.bfloat16)
        parts[1] = totals[1].astype(jnp.bfloat16)


def grads(info, starts, qd_own, ld_own, qd, ld, kv):
    return pl.pallas_call(
        grads_kernel,
        grid_spec=pltpu.PrefetchScalarGridSpec(
            num_scalar_prefetch=2,
            grid=(XS, 2),
            in_specs=[
                pl.BlockSpec(
                    (None, 2, None, ROWS, DIM),
                    lambda s, h, info, _: (info[3], 0, jnp.where(s == 0, h, 1), 0, 0),
                ),
                pl.BlockSpec((None, 8, ROWS), lambda s, h, info, _: (info[3], 0, 0)),
                pl.BlockSpec(
                    (None, 2, None, ROWS, DIM),
                    lambda s, h, *_: (jnp.maximum(s - 1, 0), 0, jnp.where(s == 0, 0, h), 0, 0),
                ),
                pl.BlockSpec((None, 8, ROWS), lambda s, h, *_: (jnp.maximum(s - 1, 0), 0, 0)),
                pl.BlockSpec(memory_space=pl.ANY),
            ],
            out_specs=[
                pl.BlockSpec((None, None, ROWS, DIM), lambda s, h, *_: (s, h, 0, 0)),
                pl.BlockSpec((2, KEY_ROWS, DIM), lambda s, h, *_: (0, 0, 0)),
            ],
            scratch_shapes=[
                pltpu.VMEM((2, KEY_ROWS, DIM), jnp.bfloat16),
                pltpu.VMEM((2, KEY_ROWS, DIM), jnp.float32),
                pltpu.VMEM((DIM, ROWS), jnp.float32),
                pltpu.VMEM((2, TILE, ROWS), jnp.bfloat16),
                pltpu.SemaphoreType.DMA,
            ],
        ),
        out_shape=(
            jax.ShapeDtypeStruct((XS, 2, ROWS, DIM), jnp.bfloat16),
            jax.ShapeDtypeStruct((2, KEY_ROWS, DIM), jnp.bfloat16),
        ),
        compiler_params=pltpu.CompilerParams(
            dimension_semantics=("arbitrary", "arbitrary"), vmem_limit_bytes=40 * 2**20
        ),
        name="grads",
    )(info, starts, qd_own, ld_own, qd, ld, kv)


def collect_kernel(
    dq_src, parts, dq, dkv, own, sib, stage, near, far, final,
    dq_send, dq_recv, own_sem, core_send, core_recv, z_send, z_recv, next_send, next_recv,
    out_send, out_recv, last_sem,
):
    window, z, x, core = place()
    greet(window, z, x, core)

    def core_copy(gid, j):
        return remote(
            piece_of(parts, gid, 1 - core, turn(x, j + 1)), sib.at[gid, j],
            core_send.at[gid, j], core_recv.at[gid, j], device(window, z, x, 1 - core),
        )

    def own_copy(gid, j):
        return pltpu.make_async_copy(piece_of(parts, gid, core, turn(x, j + 1)), own.at[gid, j], own_sem.at[gid, j])

    def dq_copy(step):
        to = turn(x, -step)
        return remote(
            dq_src.at[step], dq.at[x], dq_send.at[step - 1], dq_recv.at[step - 1], device(window, z, to, core)
        )

    def dq_arrival(step):
        came = turn(x, step)
        return remote(
            dq_src.at[step], dq.at[came], dq_send.at[step - 1], dq_recv.at[step - 1],
            device(window, z, came, core),
        )

    def out_copy(half, j):
        return remote(
            final.at[half, j], dkv.at[x, :, half],
            out_send.at[half, j], out_recv.at[half, j], device(window, z, turn(x, j + 1), core),
        )

    def out_arrival(half, j):
        came = turn(x, -j - 1)
        return remote(
            final.at[half, j], dkv.at[came, :, half],
            out_send.at[half, j], out_recv.at[half, j], device(window, z, came, core),
        )

    def out_own(half):
        return pltpu.make_async_copy(final.at[half, XS - 1], dkv.at[x, :, half], last_sem.at[1 + half])

    dq_own = pltpu.make_async_copy(dq_src.at[0], dq.at[x], last_sem.at[0])

    def z_copy(gid, j, at, way):
        return remote(
            stage.at[gid, j], near.at[gid, (1 - way) // 2, j],
            z_send.at[gid, j], z_recv.at[gid, (1 - way) // 2, j], device(window, at + way, x, core),
        )

    def next_copy(gid, j):
        return remote(
            stage.at[gid, j], far.at[j], next_send.at[gid - 8, j], next_recv.at[j],
            device(window - 1, owner_z(gid), x, core),
        )

    def next_arrival(j):
        return remote(
            stage.at[8, j], far.at[j], next_send.at[0, j], next_recv.at[j], device(window, z, x, 1 - core),
        )

    def level(at):
        order = COLLECT_ORDER[at]
        mine = (at, at + 4)

        def each(gids, act, j):
            for gid in gids:
                if gid >= 8:
                    pl.when(window > 0)(lambda: act(gid, j))
                else:
                    act(gid, j)

        def begin(gid, j):
            core_copy(gid, j).start()
            own_copy(gid, j).start()

        def towards(gid):
            owner = 0 if gid >= 8 else owner_z(gid)
            return 1 if owner > at else -1

        def summed(gid, j):
            own_copy(gid, j).wait()
            core_copy(gid, j).wait_recv()
            total = own[gid, j].astype(jnp.float32) + sib[gid, j].astype(jnp.float32)
            owner = 0 if gid >= 8 else owner_z(gid)
            for way in (-1, 1):
                came = at + way
                if 0 <= came < ZS and gid in NEED[came] and abs(came - owner) > abs(at - owner):
                    z_copy(gid, j, came, -way).wait_recv()
                    total = total + near[gid, (way + 1) // 2, j].astype(jnp.float32)
            return total

        def pass_on(gid, j):
            stage[gid, j] = summed(gid, j).astype(jnp.bfloat16)
            if gid >= 8 and at == 0:
                next_copy(gid, j).start()
            else:
                z_copy(gid, j, at, towards(gid)).start()

        def keep(half, j):
            total = summed(mine[half], j)
            if half == 0 or at not in PRIOR_FROM:
                final[half, j] = total.astype(jnp.bfloat16)
            else:

                @pl.when(window < WINDOWS - 1)
                def _():
                    next_arrival(j).wait_recv()
                    final[half, j] = (total + far[j].astype(jnp.float32)).astype(jnp.bfloat16)

                @pl.when(window == WINDOWS - 1)
                def _():
                    final[half, j] = total.astype(jnp.bfloat16)

        def finish(gid, j):
            core_copy(gid, j).wait_send()
            if gid in mine:
                return
            if gid >= 8 and at == 0:
                next_copy(gid, j).wait_send()
            else:
                z_copy(gid, j, at, towards(gid)).wait_send()

        @pl.loop(0, XS)
        def _(j):
            each((*order, *mine), begin, j)

        dq_own.start()
        for step in (2, 1, 3):
            dq_copy(step).start()
        for gid in order:
            each([gid], lambda gid, _: pl.loop(0, XS)(lambda j: pass_on(gid, j)), None)
        for half in (0, 1):

            @pl.loop(0, XS - 1)
            def _(j):
                keep(half, j)
                out_copy(half, j).start()

            keep(half, XS - 1)
            out_own(half).start()

        @pl.loop(0, XS)
        def _(j):
            each((*order, *mine), finish, j)

    for at in range(ZS):
        pl.when(z == at)(lambda at=at: level(at))

    dq_own.wait()
    for half in (0, 1):
        out_own(half).wait()
    for step in (1, 2, 3):
        dq_arrival(step).wait_recv()
        dq_copy(step).wait_send()
        for half in (0, 1):
            out_arrival(half, step - 1).wait_recv()
            out_copy(half, step - 1).wait_send()


def collect(dq_src, parts):
    dma = pltpu.SemaphoreType.DMA
    anywhere = pl.BlockSpec(memory_space=pl.ANY)
    piece = (2, BLK, DIM)
    return pl.pallas_call(
        collect_kernel,
        out_shape=(
            jax.ShapeDtypeStruct(dq_src.shape, jnp.bfloat16),
            jax.ShapeDtypeStruct((XS, 2, 2, BLK, DIM), jnp.bfloat16),
        ),
        in_specs=[anywhere] * 2,
        out_specs=[anywhere] * 2,
        scratch_shapes=[
            pltpu.VMEM((11, XS, *piece), jnp.bfloat16),
            pltpu.VMEM((11, XS, *piece), jnp.bfloat16),
            pltpu.VMEM((11, XS, *piece), jnp.bfloat16),
            pltpu.VMEM((11, 2, XS, *piece), jnp.bfloat16),
            pltpu.VMEM((XS, *piece), jnp.bfloat16),
            pltpu.VMEM((2, XS, *piece), jnp.bfloat16),
            dma((3,)), dma((3,)), dma((11, XS)), dma((11, XS)), dma((11, XS)), dma((11, XS)), dma((11, 2, XS)),
            dma((3, XS)), dma((XS,)), dma((2, XS)), dma((2, XS)), dma((3,)),
        ],
        compiler_params=pltpu.CompilerParams(
            collective_id=1, has_side_effects=True, vmem_limit_bytes=32 * 2**20
        ),
        name="collect",
    )(dq_src, parts)


def by_head(rows):
    cut = rows.reshape(2, BLK, KV, GROUP, DIM).transpose(2, 0, 3, 1, 4)
    return cut.reshape(KV, 2, ROWS, DIM)


def lanes(rows):
    return rows.reshape(KV, GROUP, 2, BLK).transpose(0, 2, 1, 3).reshape(KV, 2, ROWS)


def on_device(query, key, value, output, grad_output, lse, doc_starts):
    window, z, x, core = place()
    delta = jnp.einsum("qhd,qhd->hq", grad_output, output, preferred_element_type=jnp.float32)
    rows = jnp.stack([lanes(lse * LOG2E), lanes(delta)], axis=2).reshape(KV, 4, ROWS)
    ld_src = jnp.concatenate([rows, jnp.zeros_like(rows)], axis=1)
    qd_src = jnp.stack([by_head(query), by_head(grad_output)], axis=1)
    kv_src = jnp.stack([key, value]).reshape(2, 2, BLK, KV, DIM).transpose(3, 0, 1, 2, 4)
    kv, qd, ld = spread(kv_src, qd_src, ld_src)
    info = jnp.stack([window, z, core, x]).astype(jnp.int32)
    dq, parts = grads(info, doc_starts, qd_src, ld_src, qd, ld, kv.reshape(2, KEY_ROWS, DIM))
    dq_back, dkv = collect(dq, parts.reshape(2, PAIRS, 2, BLK, DIM))
    grad_query = (
        dq_back.reshape(KV, 2, GROUP, BLK, DIM).transpose(1, 3, 0, 2, 4).reshape(2 * BLK, KV * GROUP, DIM)
    )
    back = dkv.transpose(1, 2, 3, 0, 4).reshape(2, 2 * BLK, KV, DIM)
    return grad_query, back[0], back[1]


def solution(mesh):
    tokens = P(("outer", "inner"), None, None)
    return jax.shard_map(
        on_device,
        mesh=mesh,
        in_specs=(tokens, tokens, tokens, tokens, tokens, P(None, ("outer", "inner")), P()),
        out_specs=(tokens, tokens, tokens),
        check_vma=False,
    )
```

```python
import math

import jax
import jax.numpy as jnp
from jax import lax
from jax.experimental import pallas as pl
from jax.experimental.pallas import tpu as pltpu
from jax.sharding import PartitionSpec as P

MESH = pl.DeviceIdType.MESH
ZS, XS = 4, 4
KV, GROUP, DIM, BLK = 4, 6, 128, 64
ROWS = GROUP * BLK
WINDOWS = 8
WIN_BLOCKS = 64
WIN_ROWS = WIN_BLOCKS * BLK
PAD_PAIRS, PRIOR_PAIRS = 4, 12
BASE_PAIRS = PAD_PAIRS + PRIOR_PAIRS
PAIRS = BASE_PAIRS + WIN_BLOCKS // 2
KEY_ROWS = PAIRS * 2 * BLK
BASE_ROW = BASE_PAIRS * 2 * BLK
TILE = 512
SCALE = 1.0 / math.sqrt(DIM)
LOG2E = math.log2(math.e)

NEED = {
    0: (0, 4, 5, 2, 6, 3, 7, 8, 9, 10),
    1: (1, 5, 0, 2, 6, 3, 7, 8, 9, 10),
    2: (2, 6, 1, 3, 7, 0),
    3: (3, 7, 2, 1, 0),
}
SPREAD_ORDER = {0: (10, 9, 8, 5, 6, 2, 7, 3), 1: (6, 0, 2, 7, 3, 10, 9, 8), 2: (7, 1, 3, 0), 3: (2, 1, 0)}
COLLECT_ORDER = {0: (7, 3, 6, 2, 5, 8, 9, 10), 1: (8, 9, 10, 7, 3, 6, 2, 0), 2: (0, 1, 7, 3), 3: (0, 1, 2)}
PRIOR_FROM = (0, 1, 2)


def owner_z(gid):
    return gid % 4


def place():
    inner = lax.axis_index("inner")
    return lax.axis_index("outer"), inner // (2 * XS), (inner // 2) % XS, inner % 2


def device(window, z, x, core):
    return {"outer": window, "inner": (z * XS + x) * 2 + core}


def piece_of(ref, gid, core, x):
    z = owner_z(gid)
    if gid < 4:
        return ref.at[:, BASE_PAIRS + 4 * z + x, core]
    if gid < 8:
        return ref.at[:, BASE_PAIRS + 31 - 4 * z - x, 1 - core]
    return ref.at[:, PAD_PAIRS + 11 - 4 * z - x, 1 - core]


def block_of(ref, half, z, x, core):
    if half == 0:
        return ref.at[:, BASE_PAIRS + 4 * z + x, core]
    return ref.at[:, BASE_PAIRS + 31 - 4 * z - x, 1 - core]


def turn(x, step):
    return (x + step + XS) % XS


def has_next(window, z):
    return (window < WINDOWS - 1) & (z <= 2)


def has_previous(window, z):
    return (window > 0) & (z == 0)


def greet(window, z, x, core):
    barrier = pltpu.get_barrier_semaphore()

    def signal(*where):
        pl.semaphore_signal(barrier, inc=1, device_id=device(*where), device_id_type=MESH)

    for step in range(1, XS):
        signal(window, z, (x + step) % XS, core)
    signal(window, z, x, 1 - core)
    pl.when(z > 0)(lambda: signal(window, z - 1, x, core))
    pl.when(z < ZS - 1)(lambda: signal(window, z + 1, x, core))
    pl.when(has_next(window, z))(lambda: signal(window + 1, 0, x, core))

    @pl.when(has_previous(window, z))
    def _():
        for other in PRIOR_FROM:
            signal(window - 1, other, x, core)

    count = 4 + jnp.where(z > 0, 1, 0) + jnp.where(z < ZS - 1, 1, 0)
    count = count + jnp.where(has_next(window, z), 1, 0) + jnp.where(has_previous(window, z), 3, 0)
    pl.semaphore_wait(barrier, count)


def remote(src, dst, send, recv, where):
    return pltpu.make_async_remote_copy(
        src_ref=src, dst_ref=dst, send_sem=send, recv_sem=recv, device_id=where, device_id_type=MESH
    )


def spread_kernel(
    kv_src, qd_src, ld_src, kv, qd, ld,
    kv_send, kv_recv, qd_send, qd_recv, ld_send, ld_recv,
    z_send, z_recv, next_send, next_recv, core_send, core_recv, own_sem,
):
    window, z, x, core = place()
    greet(window, z, x, core)

    def kv_copy(step, half):
        to = turn(x, step)
        return remote(
            kv_src.at[to, :, half], block_of(kv, half, z, x, core),
            kv_send.at[step, half], kv_recv.at[step, half], device(window, z, to, core),
        )

    def kv_arrival(step, half):
        came = turn(x, -step)
        return remote(
            kv_src.at[came, :, half], block_of(kv, half, z, came, core),
            kv_send.at[step, half], kv_recv.at[step, half], device(window, z, came, core),
        )

    def wide(src, dst, send, recv, step):
        to = turn(x, step)
        return remote(
            src.at[to], dst.at[step - 1], send.at[step - 1], recv.at[step - 1], device(window, z, to, core)
        )

    for step in (2, 1, 3):
        for half in (1, 0):
            kv_copy(step, half).start()
    own = [
        pltpu.make_async_copy(kv_src.at[x, :, half], block_of(kv, half, z, x, core), own_sem.at[half])
        for half in (0, 1)
    ]

    def z_copy(gid, j, at, way, src=None):
        piece = piece_of(kv, gid, core, turn(x, -j))
        return remote(
            piece if src is None else src, piece,
            z_send.at[gid, (way + 1) // 2, j], z_recv.at[gid, j], device(window, at + way, x, core),
        )

    def next_copy(gid, j, src=None):
        piece = piece_of(kv, gid, core, turn(x, -j))
        return remote(
            piece if src is None else src, piece_of(kv, gid + 4, core, turn(x, -j)),
            next_send.at[j], next_recv.at[gid - 4, j], device(window + 1, 0, x, core),
        )

    def next_arrival(gid, j):
        piece = piece_of(kv, gid, core, turn(x, -j))
        return remote(piece, piece, next_send.at[j], next_recv.at[gid - 8, j], device(window, z, x, 1 - core))

    def core_copy(gid, j, src=None):
        piece = piece_of(kv, gid, core, turn(x, -j))
        return remote(
            piece if src is None else src, piece,
            core_send.at[gid, j], core_recv.at[gid, j], device(window, z, x, 1 - core),
        )

    def core_arrival(gid, j):
        piece = piece_of(kv, gid, 1 - core, turn(x, -j))
        return remote(piece, piece, core_send.at[gid, j], core_recv.at[gid, j], device(window, z, x, 1 - core))

    def level(at):
        def ways(gid):
            owner = 0 if gid >= 8 else owner_z(gid)
            return [
                way
                for way in (-1, 1)
                if 0 <= at + way < ZS and gid in NEED[at + way] and abs(at + way - owner) > abs(at - owner)
            ]

        def onward(gid, j, src=None):
            for way in ways(gid):
                z_copy(gid, j, at, way, src).start()
            core_copy(gid, j, src).start()

        def guarded(gid, act):
            if gid >= 8:
                pl.when(window > 0)(act)
            else:
                act()

        def given(j, src=False):
            for gid in (at + 4, at):
                first = kv_src.at[x, :, gid // 4] if src else None
                if gid >= 4 and at in PRIOR_FROM:
                    pl.when(window < WINDOWS - 1)(lambda: next_copy(gid, j, first).start())
                onward(gid, j, first)

        def arrived(gid, j):
            if gid >= 8 and at == 0:
                next_arrival(gid, j).wait_recv()
            else:
                z_copy(gid, j, at, 1 if at < ZS - 1 else -1).wait_recv()
            onward(gid, j)

        given(0, True)
        for copy in own:
            copy.start()
        for step in (2, 1, 3):
            wide(ld_src, ld, ld_send, ld_recv, step).start()
            wide(qd_src, qd, qd_send, qd_recv, step).start()

        @pl.loop(1, XS)
        def _(j):
            for half in (0, 1):
                kv_arrival(j, half).wait_recv()
            given(j)

        for gid in SPREAD_ORDER[at]:
            guarded(gid, lambda: pl.loop(0, XS)(lambda j: arrived(gid, j)))

        @pl.loop(0, XS)
        def _(j):
            for gid in NEED[at]:

                def act():
                    core_arrival(gid, j).wait_recv()
                    core_copy(gid, j).wait_send()
                    for way in ways(gid):
                        z_copy(gid, j, at, way).wait_send()

                guarded(gid, act)
            if at in PRIOR_FROM:
                pl.when(window < WINDOWS - 1)(lambda: next_copy(at + 4, j).wait_send())

    for at in range(ZS):
        pl.when(z == at)(lambda at=at: level(at))

    for copy in own:
        copy.wait()
    for step in (1, 2, 3):
        for half in (0, 1):
            kv_copy(step, half).wait_send()
        wide(ld_src, ld, ld_send, ld_recv, step).wait()
        wide(qd_src, qd, qd_send, qd_recv, step).wait()


def spread(kv_src, qd_src, ld_src):
    dma = pltpu.SemaphoreType.DMA
    anywhere = pl.BlockSpec(memory_space=pl.ANY)
    return pl.pallas_call(
        spread_kernel,
        out_shape=(
            jax.ShapeDtypeStruct((2, PAIRS, 2, BLK, DIM), jnp.bfloat16),
            jax.ShapeDtypeStruct((XS - 1, *qd_src.shape[1:]), jnp.bfloat16),
            jax.ShapeDtypeStruct((XS - 1, *ld_src.shape[1:]), jnp.float32),
        ),
        in_specs=[anywhere] * 3,
        out_specs=[anywhere] * 3,
        scratch_shapes=[
            dma((XS, 2)), dma((XS, 2)), dma((3,)), dma((3,)), dma((3,)), dma((3,)),
            dma((11, 2, XS)), dma((11, XS)), dma((XS,)), dma((3, XS)), dma((11, XS)), dma((11, XS)), dma((2,)),
        ],
        compiler_params=pltpu.CompilerParams(collective_id=0, has_side_effects=True),
        name="spread",
    )(kv_src, qd_src, ld_src)


def grads_kernel(info, starts, qd_own, ld_own, qd, ld, kv_hbm, dq, parts, kv, totals, dq_t, held, kv_sem):
    step, half = pl.program_id(0), pl.program_id(1)
    window, z, core = info[0], info[1], info[2]
    src = (info[3] - step + XS) % XS

    @pl.when((step == 0) & (half == 0))
    def _():
        load = pltpu.make_async_copy(kv_hbm, kv, kv_sem)
        load.start()
        totals[...] = jnp.zeros_like(totals)
        load.wait()

        def clear(first, blocks):
            kv[:, pl.ds(first * BLK, blocks * BLK), :] = jnp.zeros((2, blocks * BLK, DIM), jnp.bfloat16)

        clear(0, 2 * PAD_PAIRS)
        pl.when((z >= 2) | (window == 0))(lambda: clear(2 * PAD_PAIRS, 2 * PRIOR_PAIRS))
        pl.when(z == 0)(lambda: clear(2 * BASE_PAIRS + 8, 8))

    low = 8 * z + 2 * src + core
    block = jnp.where(half == 0, low, WIN_BLOCKS - 1 - low)
    shift = BASE_ROW - window * WIN_ROWS
    first = BASE_ROW + block * BLK
    query_row = first + (lax.broadcasted_iota(jnp.int32, (1, ROWS), 1) & (BLK - 1))
    query_from = jnp.zeros((1, ROWS), jnp.int32)
    begin = 0
    for entry in range(24):
        at = starts[entry] + shift
        query_from = jnp.where(query_row >= at, at, query_from)
        begin = jnp.where(first >= at, at, begin)
    end = first + BLK
    tiles = (end - begin + TILE - 1) // TILE
    q = jnp.where(step == 0, qd_own[0], qd[0])
    do = jnp.where(step == 0, qd_own[1], qd[1])
    row_at = pl.ds(2 * half, 1)
    lse = jnp.where(step == 0, ld_own[row_at, :], ld[row_at, :])
    row_at = pl.ds(2 * half + 1, 1)
    delta = jnp.where(step == 0, ld_own[row_at, :], ld[row_at, :])
    dq_t[...] = jnp.zeros_like(dq_t)

    def scores(tile):
        row = pl.multiple_of(end - (tile + 1) * TILE, BLK)
        rows = pl.ds(row, TILE)
        s = lax.dot_general(kv[0, rows, :], q, (((1,), (1,)), ((), ())), preferred_element_type=jnp.float32)
        dp = lax.dot_general(kv[1, rows, :], do, (((1,), (1,)), ((), ())), preferred_element_type=jnp.float32)
        key_row = row + lax.broadcasted_iota(jnp.int32, (TILE, 1), 0)
        allowed = (key_row <= query_row) & (key_row >= query_from)
        p = jnp.where(allowed, jnp.exp2(s * (SCALE * LOG2E) - lse), 0.0)
        return p.astype(jnp.bfloat16), (p * (dp - delta)).astype(jnp.bfloat16)

    def products(tile, p, ds):
        rows = pl.ds(pl.multiple_of(end - (tile + 1) * TILE, BLK), TILE)
        totals[1, rows, :] += jnp.dot(p, do, preferred_element_type=jnp.float32)
        totals[0, rows, :] += jnp.dot(ds, q, preferred_element_type=jnp.float32)
        dq_t[...] += lax.dot_general(kv[0, rows, :], ds, (((0,), (0,)), ((), ())), preferred_element_type=jnp.float32)

    held[0], held[1] = scores(0)

    @pl.loop(1, tiles)
    def _(tile):
        p, ds = held[0], held[1]
        new_p, new_ds = scores(tile)
        products(tile - 1, p, ds)
        held[0], held[1] = new_p, new_ds

    products(tiles - 1, held[0], held[1])

    dq[...] = (dq_t[...].T * SCALE).astype(jnp.bfloat16)

    @pl.when((step == XS - 1) & (half == 1))
    def _():
        parts[0] = (totals[0] * SCALE).astype(jnp.bfloat16)
        parts[1] = totals[1].astype(jnp.bfloat16)


def grads(info, starts, qd_own, ld_own, qd, ld, kv):
    return pl.pallas_call(
        grads_kernel,
        grid_spec=pltpu.PrefetchScalarGridSpec(
            num_scalar_prefetch=2,
            grid=(XS, 2),
            in_specs=[
                pl.BlockSpec(
                    (None, 2, None, ROWS, DIM),
                    lambda s, h, info, _: (info[3], 0, jnp.where(s == 0, h, 1), 0, 0),
                ),
                pl.BlockSpec((None, 8, ROWS), lambda s, h, info, _: (info[3], 0, 0)),
                pl.BlockSpec(
                    (None, 2, None, ROWS, DIM),
                    lambda s, h, *_: (jnp.maximum(s - 1, 0), 0, jnp.where(s == 0, 0, h), 0, 0),
                ),
                pl.BlockSpec((None, 8, ROWS), lambda s, h, *_: (jnp.maximum(s - 1, 0), 0, 0)),
                pl.BlockSpec(memory_space=pl.ANY),
            ],
            out_specs=[
                pl.BlockSpec((None, None, ROWS, DIM), lambda s, h, *_: (s, h, 0, 0)),
                pl.BlockSpec((2, KEY_ROWS, DIM), lambda s, h, *_: (0, 0, 0)),
            ],
            scratch_shapes=[
                pltpu.VMEM((2, KEY_ROWS, DIM), jnp.bfloat16),
                pltpu.VMEM((2, KEY_ROWS, DIM), jnp.float32),
                pltpu.VMEM((DIM, ROWS), jnp.float32),
                pltpu.VMEM((2, TILE, ROWS), jnp.bfloat16),
                pltpu.SemaphoreType.DMA,
            ],
        ),
        out_shape=(
            jax.ShapeDtypeStruct((XS, 2, ROWS, DIM), jnp.bfloat16),
            jax.ShapeDtypeStruct((2, KEY_ROWS, DIM), jnp.bfloat16),
        ),
        compiler_params=pltpu.CompilerParams(
            dimension_semantics=("arbitrary", "arbitrary"), vmem_limit_bytes=40 * 2**20
        ),
        name="grads",
    )(info, starts, qd_own, ld_own, qd, ld, kv)


def collect_kernel(
    dq_src, parts, dq, dkv, own, sib, stage, near, far, final,
    dq_send, dq_recv, own_sem, core_send, core_recv, z_send, z_recv, next_send, next_recv,
    out_send, out_recv, last_sem,
):
    window, z, x, core = place()
    greet(window, z, x, core)

    def core_copy(gid, j):
        return remote(
            piece_of(parts, gid, 1 - core, turn(x, j + 1)), sib.at[gid, j],
            core_send.at[gid, j], core_recv.at[gid, j], device(window, z, x, 1 - core),
        )

    def own_copy(gid, j):
        return pltpu.make_async_copy(piece_of(parts, gid, core, turn(x, j + 1)), own.at[gid, j], own_sem.at[gid, j])

    def dq_copy(step):
        to = turn(x, -step)
        return remote(
            dq_src.at[step], dq.at[x], dq_send.at[step - 1], dq_recv.at[step - 1], device(window, z, to, core)
        )

    def dq_arrival(step):
        came = turn(x, step)
        return remote(
            dq_src.at[step], dq.at[came], dq_send.at[step - 1], dq_recv.at[step - 1],
            device(window, z, came, core),
        )

    def out_copy(half, j):
        return remote(
            final.at[half, j], dkv.at[x, :, half],
            out_send.at[half, j], out_recv.at[half, j], device(window, z, turn(x, j + 1), core),
        )

    def out_arrival(half, j):
        came = turn(x, -j - 1)
        return remote(
            final.at[half, j], dkv.at[came, :, half],
            out_send.at[half, j], out_recv.at[half, j], device(window, z, came, core),
        )

    def out_own(half):
        return pltpu.make_async_copy(final.at[half, XS - 1], dkv.at[x, :, half], last_sem.at[1 + half])

    dq_own = pltpu.make_async_copy(dq_src.at[0], dq.at[x], last_sem.at[0])

    def z_copy(gid, j, at, way):
        return remote(
            stage.at[gid, j], near.at[gid, (1 - way) // 2, j],
            z_send.at[gid, j], z_recv.at[gid, (1 - way) // 2, j], device(window, at + way, x, core),
        )

    def next_copy(gid, j):
        return remote(
            stage.at[gid, j], far.at[j], next_send.at[gid - 8, j], next_recv.at[j],
            device(window - 1, owner_z(gid), x, core),
        )

    def next_arrival(j):
        return remote(
            stage.at[8, j], far.at[j], next_send.at[0, j], next_recv.at[j], device(window, z, x, 1 - core),
        )

    def level(at):
        order = COLLECT_ORDER[at]
        mine = (at, at + 4)

        def each(gids, act, j):
            for gid in gids:
                if gid >= 8:
                    pl.when(window > 0)(lambda: act(gid, j))
                else:
                    act(gid, j)

        def begin(gid, j):
            core_copy(gid, j).start()
            own_copy(gid, j).start()

        def towards(gid):
            owner = 0 if gid >= 8 else owner_z(gid)
            return 1 if owner > at else -1

        def summed(gid, j):
            own_copy(gid, j).wait()
            core_copy(gid, j).wait_recv()
            total = own[gid, j].astype(jnp.float32) + sib[gid, j].astype(jnp.float32)
            owner = 0 if gid >= 8 else owner_z(gid)
            for way in (-1, 1):
                came = at + way
                if 0 <= came < ZS and gid in NEED[came] and abs(came - owner) > abs(at - owner):
                    z_copy(gid, j, came, -way).wait_recv()
                    total = total + near[gid, (way + 1) // 2, j].astype(jnp.float32)
            return total

        def pass_on(gid, j):
            stage[gid, j] = summed(gid, j).astype(jnp.bfloat16)
            if gid >= 8 and at == 0:
                next_copy(gid, j).start()
            else:
                z_copy(gid, j, at, towards(gid)).start()

        def keep(half, j):
            total = summed(mine[half], j)
            if half == 0 or at not in PRIOR_FROM:
                final[half, j] = total.astype(jnp.bfloat16)
            else:

                @pl.when(window < WINDOWS - 1)
                def _():
                    next_arrival(j).wait_recv()
                    final[half, j] = (total + far[j].astype(jnp.float32)).astype(jnp.bfloat16)

                @pl.when(window == WINDOWS - 1)
                def _():
                    final[half, j] = total.astype(jnp.bfloat16)

        def finish(gid, j):
            core_copy(gid, j).wait_send()
            if gid in mine:
                return
            if gid >= 8 and at == 0:
                next_copy(gid, j).wait_send()
            else:
                z_copy(gid, j, at, towards(gid)).wait_send()

        @pl.loop(0, XS)
        def _(j):
            each((*order, *mine), begin, j)

        dq_own.start()
        for step in (2, 1, 3):
            dq_copy(step).start()
        for gid in order:
            each([gid], lambda gid, _: pl.loop(0, XS)(lambda j: pass_on(gid, j)), None)
        for half in (0, 1):

            @pl.loop(0, XS - 1)
            def _(j):
                keep(half, j)
                out_copy(half, j).start()

            keep(half, XS - 1)
            out_own(half).start()

        @pl.loop(0, XS)
        def _(j):
            each((*order, *mine), finish, j)

    for at in range(ZS):
        pl.when(z == at)(lambda at=at: level(at))

    dq_own.wait()
    for half in (0, 1):
        out_own(half).wait()
    for step in (1, 2, 3):
        dq_arrival(step).wait_recv()
        dq_copy(step).wait_send()
        for half in (0, 1):
            out_arrival(half, step - 1).wait_recv()
            out_copy(half, step - 1).wait_send()


def collect(dq_src, parts):
    dma = pltpu.SemaphoreType.DMA
    anywhere = pl.BlockSpec(memory_space=pl.ANY)
    piece = (2, BLK, DIM)
    return pl.pallas_call(
        collect_kernel,
        out_shape=(
            jax.ShapeDtypeStruct(dq_src.shape, jnp.bfloat16),
            jax.ShapeDtypeStruct((XS, 2, 2, BLK, DIM), jnp.bfloat16),
        ),
        in_specs=[anywhere] * 2,
        out_specs=[anywhere] * 2,
        scratch_shapes=[
            pltpu.VMEM((11, XS, *piece), jnp.bfloat16),
            pltpu.VMEM((11, XS, *piece), jnp.bfloat16),
            pltpu.VMEM((11, XS, *piece), jnp.bfloat16),
            pltpu.VMEM((11, 2, XS, *piece), jnp.bfloat16),
            pltpu.VMEM((XS, *piece), jnp.bfloat16),
            pltpu.VMEM((2, XS, *piece), jnp.bfloat16),
            dma((3,)), dma((3,)), dma((11, XS)), dma((11, XS)), dma((11, XS)), dma((11, XS)), dma((11, 2, XS)),
            dma((3, XS)), dma((XS,)), dma((2, XS)), dma((2, XS)), dma((3,)),
        ],
        compiler_params=pltpu.CompilerParams(
            collective_id=1, has_side_effects=True, vmem_limit_bytes=32 * 2**20
        ),
        name="collect",
    )(dq_src, parts)


def by_head(rows):
    cut = rows.reshape(2, BLK, KV, GROUP, DIM).transpose(2, 0, 3, 1, 4)
    return cut.reshape(KV, 2, ROWS, DIM)


def lanes(rows):
    return rows.reshape(KV, GROUP, 2, BLK).transpose(0, 2, 1, 3).reshape(KV, 2, ROWS)


def on_device(query, key, value, output, grad_output, lse, doc_starts):
    window, z, x, core = place()
    delta = jnp.einsum("qhd,qhd->hq", grad_output, output, preferred_element_type=jnp.float32)
    rows = jnp.stack([lanes(lse * LOG2E), lanes(delta)], axis=2).reshape(KV, 4, ROWS)
    ld_src = jnp.concatenate([rows, jnp.zeros_like(rows)], axis=1)
    qd_src = jnp.stack([by_head(query), by_head(grad_output)], axis=1)
    kv_src = jnp.stack([key, value]).reshape(2, 2, BLK, KV, DIM).transpose(3, 0, 1, 2, 4)
    kv, qd, ld = spread(kv_src, qd_src, ld_src)
    info = jnp.stack([window, z, core, x]).astype(jnp.int32)
    dq, parts = grads(info, doc_starts, qd_src, ld_src, qd, ld, kv.reshape(2, KEY_ROWS, DIM))
    dq_back, dkv = collect(dq, parts.reshape(2, PAIRS, 2, BLK, DIM))
    grad_query = (
        dq_back.reshape(KV, 2, GROUP, BLK, DIM).transpose(1, 3, 0, 2, 4).reshape(2 * BLK, KV * GROUP, DIM)
    )
    back = dkv.transpose(1, 2, 3, 0, 4).reshape(2, 2 * BLK, KV, DIM)
    return grad_query, back[0], back[1]


def solution(mesh):
    tokens = P(("outer", "inner"), None, None)
    return jax.shard_map(
        on_device,
        mesh=mesh,
        in_specs=(tokens, tokens, tokens, tokens, tokens, P(None, ("outer", "inner")), P()),
        out_specs=(tokens, tokens, tokens),
        check_vma=False,
    )
```

```python
import math

import jax
import jax.numpy as jnp
from jax import lax
from jax.experimental import pallas as pl
from jax.experimental.pallas import tpu as pltpu
from jax.sharding import PartitionSpec as P

MESH = pl.DeviceIdType.MESH
ZS, XS = 4, 4
KV, GROUP, DIM, BLK = 4, 6, 128, 64
ROWS = GROUP * BLK
WINDOWS = 8
WIN_BLOCKS = 64
WIN_ROWS = WIN_BLOCKS * BLK
PAD_PAIRS, PRIOR_PAIRS = 2, 12
BASE_PAIRS = PAD_PAIRS + PRIOR_PAIRS
PAIRS = BASE_PAIRS + WIN_BLOCKS // 2
KEY_ROWS = PAIRS * 2 * BLK
BASE_ROW = BASE_PAIRS * 2 * BLK
TILE = 256
SCALE = 1.0 / math.sqrt(DIM)
LOG2E = math.log2(math.e)

NEED = {
    0: (0, 4, 5, 2, 6, 3, 7, 8, 9, 10),
    1: (1, 5, 0, 2, 6, 3, 7, 8, 9, 10),
    2: (2, 6, 1, 3, 7, 0),
    3: (3, 7, 2, 1, 0),
}
SPREAD_ORDER = {0: (10, 9, 8, 5, 6, 2, 7, 3), 1: (6, 0, 2, 7, 3, 10, 9, 8), 2: (7, 1, 3, 0), 3: (2, 1, 0)}
COLLECT_ORDER = {0: (7, 3, 6, 2, 5, 8, 9, 10), 1: (8, 9, 10, 7, 3, 6, 2, 0), 2: (0, 1, 7, 3), 3: (0, 1, 2)}
PRIOR_FROM = (0, 1, 2)


def owner_z(gid):
    return gid % 4


def place():
    inner = lax.axis_index("inner")
    return lax.axis_index("outer"), inner // (2 * XS), (inner // 2) % XS, inner % 2


def device(window, z, x, core):
    return {"outer": window, "inner": (z * XS + x) * 2 + core}


def piece_of(ref, gid, core, x):
    z = owner_z(gid)
    if gid < 4:
        return ref.at[:, BASE_PAIRS + 4 * z + x, core]
    if gid < 8:
        return ref.at[:, BASE_PAIRS + 31 - 4 * z - x, 1 - core]
    return ref.at[:, PAD_PAIRS + 11 - 4 * z - x, 1 - core]


def block_of(ref, half, z, x, core):
    if half == 0:
        return ref.at[:, BASE_PAIRS + 4 * z + x, core]
    return ref.at[:, BASE_PAIRS + 31 - 4 * z - x, 1 - core]


def turn(x, step):
    return (x + step + XS) % XS


def has_next(window, z):
    return (window < WINDOWS - 1) & (z <= 2)


def has_previous(window, z):
    return (window > 0) & (z == 0)


def greet(window, z, x, core):
    barrier = pltpu.get_barrier_semaphore()

    def signal(*where):
        pl.semaphore_signal(barrier, inc=1, device_id=device(*where), device_id_type=MESH)

    for step in range(1, XS):
        signal(window, z, (x + step) % XS, core)
    signal(window, z, x, 1 - core)
    pl.when(z > 0)(lambda: signal(window, z - 1, x, core))
    pl.when(z < ZS - 1)(lambda: signal(window, z + 1, x, core))
    pl.when(has_next(window, z))(lambda: signal(window + 1, 0, x, core))

    @pl.when(has_previous(window, z))
    def _():
        for other in PRIOR_FROM:
            signal(window - 1, other, x, core)

    count = 4 + jnp.where(z > 0, 1, 0) + jnp.where(z < ZS - 1, 1, 0)
    count = count + jnp.where(has_next(window, z), 1, 0) + jnp.where(has_previous(window, z), 3, 0)
    pl.semaphore_wait(barrier, count)


def remote(src, dst, send, recv, where):
    return pltpu.make_async_remote_copy(
        src_ref=src, dst_ref=dst, send_sem=send, recv_sem=recv, device_id=where, device_id_type=MESH
    )


def spread_kernel(
    kv_src, qd_src, ld_src, kv, qd, ld,
    kv_send, kv_recv, qd_send, qd_recv, ld_send, ld_recv,
    z_send, z_recv, next_send, next_recv, core_send, core_recv, own_sem,
):
    window, z, x, core = place()
    greet(window, z, x, core)

    def kv_copy(step, half):
        to = turn(x, step)
        return remote(
            kv_src.at[to, :, half], block_of(kv, half, z, x, core),
            kv_send.at[step, half], kv_recv.at[step, half], device(window, z, to, core),
        )

    def kv_arrival(step, half):
        came = turn(x, -step)
        return remote(
            kv_src.at[came, :, half], block_of(kv, half, z, came, core),
            kv_send.at[step, half], kv_recv.at[step, half], device(window, z, came, core),
        )

    def wide(src, dst, send, recv, step):
        to = turn(x, step)
        return remote(
            src.at[to], dst.at[step - 1], send.at[step - 1], recv.at[step - 1], device(window, z, to, core)
        )

    for step in (2, 1, 3):
        for half in (1, 0):
            kv_copy(step, half).start()
    own = [
        pltpu.make_async_copy(kv_src.at[x, :, half], block_of(kv, half, z, x, core), own_sem.at[half])
        for half in (0, 1)
    ]

    def z_copy(gid, j, at, way, src=None):
        piece = piece_of(kv, gid, core, turn(x, -j))
        return remote(
            piece if src is None else src, piece,
            z_send.at[gid, (way + 1) // 2, j], z_recv.at[gid, j], device(window, at + way, x, core),
        )

    def next_copy(gid, j, src=None):
        piece = piece_of(kv, gid, core, turn(x, -j))
        return remote(
            piece if src is None else src, piece_of(kv, gid + 4, core, turn(x, -j)),
            next_send.at[j], next_recv.at[gid - 4, j], device(window + 1, 0, x, core),
        )

    def next_arrival(gid, j):
        piece = piece_of(kv, gid, core, turn(x, -j))
        return remote(piece, piece, next_send.at[j], next_recv.at[gid - 8, j], device(window, z, x, 1 - core))

    def core_copy(gid, j, src=None):
        piece = piece_of(kv, gid, core, turn(x, -j))
        return remote(
            piece if src is None else src, piece,
            core_send.at[gid, j], core_recv.at[gid, j], device(window, z, x, 1 - core),
        )

    def core_arrival(gid, j):
        piece = piece_of(kv, gid, 1 - core, turn(x, -j))
        return remote(piece, piece, core_send.at[gid, j], core_recv.at[gid, j], device(window, z, x, 1 - core))

    def level(at):
        def ways(gid):
            owner = 0 if gid >= 8 else owner_z(gid)
            return [
                way
                for way in (-1, 1)
                if 0 <= at + way < ZS and gid in NEED[at + way] and abs(at + way - owner) > abs(at - owner)
            ]

        def onward(gid, j, src=None):
            for way in ways(gid):
                z_copy(gid, j, at, way, src).start()
            core_copy(gid, j, src).start()

        def guarded(gid, act):
            if gid >= 8:
                pl.when(window > 0)(act)
            else:
                act()

        def given(j, src=False):
            for gid in (at + 4, at):
                first = kv_src.at[x, :, gid // 4] if src else None
                if gid >= 4 and at in PRIOR_FROM:
                    pl.when(window < WINDOWS - 1)(lambda: next_copy(gid, j, first).start())
                onward(gid, j, first)

        def arrived(gid, j):
            if gid >= 8 and at == 0:
                next_arrival(gid, j).wait_recv()
            else:
                z_copy(gid, j, at, 1 if at < ZS - 1 else -1).wait_recv()
            onward(gid, j)

        given(0, True)
        for copy in own:
            copy.start()
        for step in (2, 1, 3):
            wide(ld_src, ld, ld_send, ld_recv, step).start()
            wide(qd_src, qd, qd_send, qd_recv, step).start()

        @pl.loop(1, XS)
        def _(j):
            for half in (0, 1):
                kv_arrival(j, half).wait_recv()
            given(j)

        for gid in SPREAD_ORDER[at]:
            guarded(gid, lambda: pl.loop(0, XS)(lambda j: arrived(gid, j)))

        @pl.loop(0, XS)
        def _(j):
            for gid in NEED[at]:

                def act():
                    core_arrival(gid, j).wait_recv()
                    core_copy(gid, j).wait_send()
                    for way in ways(gid):
                        z_copy(gid, j, at, way).wait_send()

                guarded(gid, act)
            if at in PRIOR_FROM:
                pl.when(window < WINDOWS - 1)(lambda: next_copy(at + 4, j).wait_send())

    for at in range(ZS):
        pl.when(z == at)(lambda at=at: level(at))

    for copy in own:
        copy.wait()
    for step in (1, 2, 3):
        for half in (0, 1):
            kv_copy(step, half).wait_send()
        wide(ld_src, ld, ld_send, ld_recv, step).wait()
        wide(qd_src, qd, qd_send, qd_recv, step).wait()


def spread(kv_src, qd_src, ld_src):
    dma = pltpu.SemaphoreType.DMA
    anywhere = pl.BlockSpec(memory_space=pl.ANY)
    return pl.pallas_call(
        spread_kernel,
        out_shape=(
            jax.ShapeDtypeStruct((2, PAIRS, 2, BLK, DIM), jnp.bfloat16),
            jax.ShapeDtypeStruct((XS - 1, *qd_src.shape[1:]), jnp.bfloat16),
            jax.ShapeDtypeStruct((XS - 1, *ld_src.shape[1:]), jnp.float32),
        ),
        in_specs=[anywhere] * 3,
        out_specs=[anywhere] * 3,
        scratch_shapes=[
            dma((XS, 2)), dma((XS, 2)), dma((3,)), dma((3,)), dma((3,)), dma((3,)),
            dma((11, 2, XS)), dma((11, XS)), dma((XS,)), dma((3, XS)), dma((11, XS)), dma((11, XS)), dma((2,)),
        ],
        compiler_params=pltpu.CompilerParams(collective_id=0, has_side_effects=True),
        name="spread",
    )(kv_src, qd_src, ld_src)


def grads_kernel(
    info, starts, qd_own, ld_own, qd_a, ld_a, qd_b, ld_b, kv_hbm, dq, parts,
    kv, totals, dq_t, held, q, do, kv_sem,
):
    pair, half = pl.program_id(0), pl.program_id(1)
    window, z, core, x = info[0], info[1], info[2], info[3]
    slot_a, slot_b = (x - 2 * pair) & 3, (x - 2 * pair - 1) & 3

    @pl.when((pair == 0) & (half == 0))
    def _():
        load = pltpu.make_async_copy(kv_hbm, kv, kv_sem)
        load.start()
        totals[...] = jnp.zeros_like(totals)
        load.wait()

        def clear(first, blocks):
            kv[:, pl.ds(first * BLK, blocks * BLK), :] = jnp.zeros((2, blocks * BLK, DIM), jnp.bfloat16)

        clear(0, 2 * PAD_PAIRS)
        pl.when((z >= 2) | (window == 0))(lambda: clear(2 * PAD_PAIRS, 2 * PRIOR_PAIRS))
        pl.when(z == 0)(lambda: clear(2 * BASE_PAIRS + 8, 8))

    low = 8 * z + 4 * pair + core
    block_a = jnp.where(half == 0, low, WIN_BLOCKS - 1 - low)
    block_b = jnp.where(half == 0, low + 2, WIN_BLOCKS - 3 - low)
    shift = BASE_ROW - window * WIN_ROWS
    first = BASE_ROW + jnp.minimum(block_a, block_b) * BLK
    lane = lax.broadcasted_iota(jnp.int32, (1, 2 * ROWS), 1)
    query_row = BASE_ROW + jnp.where(lane < ROWS, block_a, block_b) * BLK + (lane & (BLK - 1))
    query_from = jnp.zeros((1, 2 * ROWS), jnp.int32)
    begin = 0
    for entry in range(24):
        at = starts[entry] + shift
        query_from = jnp.where(query_row >= at, at, query_from)
        begin = jnp.where(first >= at, at, begin)
    end = first + 3 * BLK
    tiles = (end - begin + TILE - 1) // TILE
    for at, slot, came in ((0, slot_a, qd_a), (ROWS, slot_b, qd_b)):
        q[pl.ds(at, ROWS), :] = jnp.where(slot == 0, qd_own[0], came[0])
        do[pl.ds(at, ROWS), :] = jnp.where(slot == 0, qd_own[1], came[1])

    def lanes_of(row):
        at = pl.ds(2 * half + row, 1)
        return jnp.concatenate(
            [jnp.where(slot == 0, ld_own[at, :], came[at, :]) for slot, came in ((slot_a, ld_a), (slot_b, ld_b))],
            axis=1,
        )

    lse, delta = lanes_of(0), lanes_of(1)
    dq_t[...] = jnp.zeros_like(dq_t)

    def scores(tile):
        row = pl.multiple_of(end - (tile + 1) * TILE, BLK)
        rows = pl.ds(row, TILE)
        s = lax.dot_general(kv[0, rows, :], q[...], (((1,), (1,)), ((), ())), preferred_element_type=jnp.float32)
        dp = lax.dot_general(kv[1, rows, :], do[...], (((1,), (1,)), ((), ())), preferred_element_type=jnp.float32)
        key_row = row + lax.broadcasted_iota(jnp.int32, (TILE, 1), 0)
        allowed = (key_row <= query_row) & (key_row >= query_from)
        p = jnp.where(allowed, jnp.exp2(s * (SCALE * LOG2E) - lse), 0.0)
        return p.astype(jnp.bfloat16), (p * (dp - delta)).astype(jnp.bfloat16)

    def products(tile, p, ds):
        rows = pl.ds(pl.multiple_of(end - (tile + 1) * TILE, BLK), TILE)
        totals[1, rows, :] += jnp.dot(p, do[...], preferred_element_type=jnp.float32)
        totals[0, rows, :] += jnp.dot(ds, q[...], preferred_element_type=jnp.float32)
        dq_t[...] += lax.dot_general(kv[0, rows, :], ds, (((0,), (0,)), ((), ())), preferred_element_type=jnp.float32)

    held[0], held[1] = scores(0)

    @pl.loop(1, tiles)
    def _(tile):
        p, ds = held[0], held[1]
        new_p, new_ds = scores(tile)
        products(tile - 1, p, ds)
        held[0], held[1] = new_p, new_ds

    products(tiles - 1, held[0], held[1])

    rows_out = (dq_t[...].T * SCALE).astype(jnp.bfloat16)
    dq[slot_a, half] = rows_out[:ROWS]
    dq[slot_b, half] = rows_out[ROWS:]

    @pl.when((pair == 1) & (half == 1))
    def _():
        parts[0] = (totals[0] * SCALE).astype(jnp.bfloat16)
        parts[1] = totals[1].astype(jnp.bfloat16)


def slot_at(info, pair, second):
    return jnp.maximum(((info[3] - 2 * pair - second) & 3) - 1, 0)


def grads(info, starts, qd_own, ld_own, qd, ld, kv):
    return pl.pallas_call(
        grads_kernel,
        grid_spec=pltpu.PrefetchScalarGridSpec(
            num_scalar_prefetch=2,
            grid=(2, 2),
            in_specs=[
                pl.BlockSpec((None, 2, None, ROWS, DIM), lambda s, h, info, _: (info[3], 0, h, 0, 0)),
                pl.BlockSpec((None, 8, ROWS), lambda s, h, info, _: (info[3], 0, 0)),
                *(
                    spec
                    for second in (0, 1)
                    for spec in (
                        pl.BlockSpec(
                            (None, 2, None, ROWS, DIM),
                            lambda s, h, info, _, second=second: (slot_at(info, s, second), 0, h, 0, 0),
                        ),
                        pl.BlockSpec(
                            (None, 8, ROWS),
                            lambda s, h, info, _, second=second: (slot_at(info, s, second), 0, 0),
                        ),
                    )
                ),
                pl.BlockSpec(memory_space=pl.ANY),
            ],
            out_specs=[
                pl.BlockSpec((XS, 2, ROWS, DIM), lambda s, h, *_: (0, 0, 0, 0)),
                pl.BlockSpec((2, KEY_ROWS, DIM), lambda s, h, *_: (0, 0, 0)),
            ],
            scratch_shapes=[
                pltpu.VMEM((2, KEY_ROWS, DIM), jnp.bfloat16),
                pltpu.VMEM((2, KEY_ROWS, DIM), jnp.float32),
                pltpu.VMEM((DIM, 2 * ROWS), jnp.float32),
                pltpu.VMEM((2, TILE, 2 * ROWS), jnp.bfloat16),
                pltpu.VMEM((2 * ROWS, DIM), jnp.bfloat16),
                pltpu.VMEM((2 * ROWS, DIM), jnp.bfloat16),
                pltpu.SemaphoreType.DMA,
            ],
        ),
        out_shape=(
            jax.ShapeDtypeStruct((XS, 2, ROWS, DIM), jnp.bfloat16),
            jax.ShapeDtypeStruct((2, KEY_ROWS, DIM), jnp.bfloat16),
        ),
        compiler_params=pltpu.CompilerParams(
            dimension_semantics=("arbitrary", "arbitrary"), vmem_limit_bytes=40 * 2**20
        ),
        name="grads",
    )(info, starts, qd_own, ld_own, qd, ld, qd, ld, kv)


def collect_kernel(
    dq_src, parts, dq, dkv, own, sib, stage, near, far, final,
    dq_send, dq_recv, own_sem, core_send, core_recv, z_send, z_recv, next_send, next_recv,
    out_send, out_recv, last_sem,
):
    window, z, x, core = place()
    greet(window, z, x, core)

    def core_copy(gid, j):
        return remote(
            piece_of(parts, gid, 1 - core, turn(x, j + 1)), sib.at[gid, j],
            core_send.at[gid, j], core_recv.at[gid, j], device(window, z, x, 1 - core),
        )

    def own_copy(gid, j):
        return pltpu.make_async_copy(piece_of(parts, gid, core, turn(x, j + 1)), own.at[gid, j], own_sem.at[gid, j])

    def dq_copy(step):
        to = turn(x, -step)
        return remote(
            dq_src.at[step], dq.at[x], dq_send.at[step - 1], dq_recv.at[step - 1], device(window, z, to, core)
        )

    def dq_arrival(step):
        came = turn(x, step)
        return remote(
            dq_src.at[step], dq.at[came], dq_send.at[step - 1], dq_recv.at[step - 1],
            device(window, z, came, core),
        )

    def out_copy(half, j):
        return remote(
            final.at[half, j], dkv.at[x, :, half],
            out_send.at[half, j], out_recv.at[half, j], device(window, z, turn(x, j + 1), core),
        )

    def out_arrival(half, j):
        came = turn(x, -j - 1)
        return remote(
            final.at[half, j], dkv.at[came, :, half],
            out_send.at[half, j], out_recv.at[half, j], device(window, z, came, core),
        )

    def out_own(half):
        return pltpu.make_async_copy(final.at[half, XS - 1], dkv.at[x, :, half], last_sem.at[1 + half])

    dq_own = pltpu.make_async_copy(dq_src.at[0], dq.at[x], last_sem.at[0])

    def z_copy(gid, j, at, way):
        return remote(
            stage.at[gid, j], near.at[gid, (1 - way) // 2, j],
            z_send.at[gid, j], z_recv.at[gid, (1 - way) // 2, j], device(window, at + way, x, core),
        )

    def next_copy(gid, j):
        return remote(
            stage.at[gid, j], far.at[j], next_send.at[gid - 8, j], next_recv.at[j],
            device(window - 1, owner_z(gid), x, core),
        )

    def next_arrival(j):
        return remote(
            stage.at[8, j], far.at[j], next_send.at[0, j], next_recv.at[j], device(window, z, x, 1 - core),
        )

    def level(at):
        order = COLLECT_ORDER[at]
        mine = (at, at + 4)

        def each(gids, act, j):
            for gid in gids:
                if gid >= 8:
                    pl.when(window > 0)(lambda: act(gid, j))
                else:
                    act(gid, j)

        def begin(gid, j):
            core_copy(gid, j).start()
            own_copy(gid, j).start()

        def towards(gid):
            owner = 0 if gid >= 8 else owner_z(gid)
            return 1 if owner > at else -1

        def summed(gid, j):
            own_copy(gid, j).wait()
            core_copy(gid, j).wait_recv()
            total = own[gid, j].astype(jnp.float32) + sib[gid, j].astype(jnp.float32)
            owner = 0 if gid >= 8 else owner_z(gid)
            for way in (-1, 1):
                came = at + way
                if 0 <= came < ZS and gid in NEED[came] and abs(came - owner) > abs(at - owner):
                    z_copy(gid, j, came, -way).wait_recv()
                    total = total + near[gid, (way + 1) // 2, j].astype(jnp.float32)
            return total

        def pass_on(gid, j):
            stage[gid, j] = summed(gid, j).astype(jnp.bfloat16)
            if gid >= 8 and at == 0:
                next_copy(gid, j).start()
            else:
                z_copy(gid, j, at, towards(gid)).start()

        def keep(half, j):
            total = summed(mine[half], j)
            if half == 0 or at not in PRIOR_FROM:
                final[half, j] = total.astype(jnp.bfloat16)
            else:

                @pl.when(window < WINDOWS - 1)
                def _():
                    next_arrival(j).wait_recv()
                    final[half, j] = (total + far[j].astype(jnp.float32)).astype(jnp.bfloat16)

                @pl.when(window == WINDOWS - 1)
                def _():
                    final[half, j] = total.astype(jnp.bfloat16)

        def finish(gid, j):
            core_copy(gid, j).wait_send()
            if gid in mine:
                return
            if gid >= 8 and at == 0:
                next_copy(gid, j).wait_send()
            else:
                z_copy(gid, j, at, towards(gid)).wait_send()

        @pl.loop(0, XS)
        def _(j):
            each((*order, *mine), begin, j)

        dq_own.start()
        for step in (2, 1, 3):
            dq_copy(step).start()
        for gid in order:
            each([gid], lambda gid, _: pl.loop(0, XS)(lambda j: pass_on(gid, j)), None)
        for half in (0, 1):

            @pl.loop(0, XS - 1)
            def _(j):
                keep(half, j)
                out_copy(half, j).start()

            keep(half, XS - 1)
            out_own(half).start()

        @pl.loop(0, XS)
        def _(j):
            each((*order, *mine), finish, j)

    for at in range(ZS):
        pl.when(z == at)(lambda at=at: level(at))

    dq_own.wait()
    for half in (0, 1):
        out_own(half).wait()
    for step in (1, 2, 3):
        dq_arrival(step).wait_recv()
        dq_copy(step).wait_send()
        for half in (0, 1):
            out_arrival(half, step - 1).wait_recv()
            out_copy(half, step - 1).wait_send()


def collect(dq_src, parts):
    dma = pltpu.SemaphoreType.DMA
    anywhere = pl.BlockSpec(memory_space=pl.ANY)
    piece = (2, BLK, DIM)
    return pl.pallas_call(
        collect_kernel,
        out_shape=(
            jax.ShapeDtypeStruct(dq_src.shape, jnp.bfloat16),
            jax.ShapeDtypeStruct((XS, 2, 2, BLK, DIM), jnp.bfloat16),
        ),
        in_specs=[anywhere] * 2,
        out_specs=[anywhere] * 2,
        scratch_shapes=[
            pltpu.VMEM((11, XS, *piece), jnp.bfloat16),
            pltpu.VMEM((11, XS, *piece), jnp.bfloat16),
            pltpu.VMEM((11, XS, *piece), jnp.bfloat16),
            pltpu.VMEM((11, 2, XS, *piece), jnp.bfloat16),
            pltpu.VMEM((XS, *piece), jnp.bfloat16),
            pltpu.VMEM((2, XS, *piece), jnp.bfloat16),
            dma((3,)), dma((3,)), dma((11, XS)), dma((11, XS)), dma((11, XS)), dma((11, XS)), dma((11, 2, XS)),
            dma((3, XS)), dma((XS,)), dma((2, XS)), dma((2, XS)), dma((3,)),
        ],
        compiler_params=pltpu.CompilerParams(
            collective_id=1, has_side_effects=True, vmem_limit_bytes=32 * 2**20
        ),
        name="collect",
    )(dq_src, parts)


def by_head(rows):
    cut = rows.reshape(2, BLK, KV, GROUP, DIM).transpose(2, 0, 3, 1, 4)
    return cut.reshape(KV, 2, ROWS, DIM)


def lanes(rows):
    return rows.reshape(KV, GROUP, 2, BLK).transpose(0, 2, 1, 3).reshape(KV, 2, ROWS)


def on_device(query, key, value, output, grad_output, lse, doc_starts):
    window, z, x, core = place()
    delta = jnp.einsum("qhd,qhd->hq", grad_output, output, preferred_element_type=jnp.float32)
    rows = jnp.stack([lanes(lse * LOG2E), lanes(delta)], axis=2).reshape(KV, 4, ROWS)
    ld_src = jnp.concatenate([rows, jnp.zeros_like(rows)], axis=1)
    qd_src = jnp.stack([by_head(query), by_head(grad_output)], axis=1)
    kv_src = jnp.stack([key, value]).reshape(2, 2, BLK, KV, DIM).transpose(3, 0, 1, 2, 4)
    kv, qd, ld = spread(kv_src, qd_src, ld_src)
    info = jnp.stack([window, z, core, x]).astype(jnp.int32)
    dq, parts = grads(info, doc_starts, qd_src, ld_src, qd, ld, kv.reshape(2, KEY_ROWS, DIM))
    dq_back, dkv = collect(dq, parts.reshape(2, PAIRS, 2, BLK, DIM))
    grad_query = (
        dq_back.reshape(KV, 2, GROUP, BLK, DIM).transpose(1, 3, 0, 2, 4).reshape(2 * BLK, KV * GROUP, DIM)
    )
    back = dkv.transpose(1, 2, 3, 0, 4).reshape(2, 2 * BLK, KV, DIM)
    return grad_query, back[0], back[1]


def solution(mesh):
    tokens = P(("outer", "inner"), None, None)
    return jax.shard_map(
        on_device,
        mesh=mesh,
        in_specs=(tokens, tokens, tokens, tokens, tokens, P(None, ("outer", "inner")), P()),
        out_specs=(tokens, tokens, tokens),
        check_vma=False,
    )
```

```python
import math

import jax
import jax.numpy as jnp
from jax import lax
from jax.experimental import pallas as pl
from jax.experimental.pallas import tpu as pltpu
from jax.sharding import PartitionSpec as P

MESH = pl.DeviceIdType.MESH
ZS, XS = 4, 4
KV, GROUP, DIM, BLK = 4, 6, 128, 64
ROWS = GROUP * BLK
WINDOWS = 8
WIN_BLOCKS = 64
WIN_ROWS = WIN_BLOCKS * BLK
PAD_PAIRS, PRIOR_PAIRS = 2, 12
BASE_PAIRS = PAD_PAIRS + PRIOR_PAIRS
PAIRS = BASE_PAIRS + WIN_BLOCKS // 2
KEY_ROWS = PAIRS * 2 * BLK
BASE_ROW = BASE_PAIRS * 2 * BLK
TILE = 256
SCALE = 1.0 / math.sqrt(DIM)
LOG2E = math.log2(math.e)

NEED = {
    0: (0, 4, 5, 2, 6, 3, 7, 8, 9, 10),
    1: (1, 5, 0, 2, 6, 3, 7, 8, 9, 10),
    2: (2, 6, 1, 3, 7, 0),
    3: (3, 7, 2, 1, 0),
}
SPREAD_ORDER = {0: (10, 9, 8, 5, 6, 2, 7, 3), 1: (6, 0, 2, 7, 3, 10, 9, 8), 2: (7, 1, 3, 0), 3: (2, 1, 0)}
COLLECT_ORDER = {0: (7, 3, 6, 2, 5, 8, 9, 10), 1: (8, 9, 10, 7, 3, 6, 2, 0), 2: (0, 1, 7, 3), 3: (0, 1, 2)}
PRIOR_FROM = (0, 1, 2)


def owner_z(gid):
    return gid % 4


def place():
    inner = lax.axis_index("inner")
    return lax.axis_index("outer"), inner // (2 * XS), (inner // 2) % XS, inner % 2


def device(window, z, x, core):
    return {"outer": window, "inner": (z * XS + x) * 2 + core}


def piece_of(ref, gid, core, x):
    z = owner_z(gid)
    if gid < 4:
        return ref.at[:, BASE_PAIRS + 4 * z + x, core]
    if gid < 8:
        return ref.at[:, BASE_PAIRS + 31 - 4 * z - x, 1 - core]
    return ref.at[:, PAD_PAIRS + 11 - 4 * z - x, 1 - core]


def block_of(ref, half, z, x, core):
    if half == 0:
        return ref.at[:, BASE_PAIRS + 4 * z + x, core]
    return ref.at[:, BASE_PAIRS + 31 - 4 * z - x, 1 - core]


def turn(x, step):
    return (x + step + XS) % XS


def has_next(window, z):
    return (window < WINDOWS - 1) & (z <= 2)


def has_previous(window, z):
    return (window > 0) & (z == 0)


def greet(window, z, x, core):
    barrier = pltpu.get_barrier_semaphore()

    def signal(*where):
        pl.semaphore_signal(barrier, inc=1, device_id=device(*where), device_id_type=MESH)

    for step in range(1, XS):
        signal(window, z, (x + step) % XS, core)
    signal(window, z, x, 1 - core)
    pl.when(z > 0)(lambda: signal(window, z - 1, x, core))
    pl.when(z < ZS - 1)(lambda: signal(window, z + 1, x, core))
    pl.when(has_next(window, z))(lambda: signal(window + 1, 0, x, core))

    @pl.when(has_previous(window, z))
    def _():
        for other in PRIOR_FROM:
            signal(window - 1, other, x, core)

    count = 4 + jnp.where(z > 0, 1, 0) + jnp.where(z < ZS - 1, 1, 0)
    count = count + jnp.where(has_next(window, z), 1, 0) + jnp.where(has_previous(window, z), 3, 0)
    pl.semaphore_wait(barrier, count)


def remote(src, dst, send, recv, where):
    return pltpu.make_async_remote_copy(
        src_ref=src, dst_ref=dst, send_sem=send, recv_sem=recv, device_id=where, device_id_type=MESH
    )


def spread_kernel(
    kv_src, qd_src, ld_src, kv, qd, ld,
    kv_send, kv_recv, qd_send, qd_recv, ld_send, ld_recv,
    z_send, z_recv, next_send, next_recv, core_send, core_recv, own_sem,
):
    window, z, x, core = place()
    greet(window, z, x, core)

    def kv_copy(step, half):
        to = turn(x, step)
        return remote(
            kv_src.at[to, :, half], block_of(kv, half, z, x, core),
            kv_send.at[step, half], kv_recv.at[step, half], device(window, z, to, core),
        )

    def kv_arrival(step, half):
        came = turn(x, -step)
        return remote(
            kv_src.at[came, :, half], block_of(kv, half, z, came, core),
            kv_send.at[step, half], kv_recv.at[step, half], device(window, z, came, core),
        )

    def wide(src, dst, send, recv, step):
        to = turn(x, step)
        return remote(
            src.at[to], dst.at[step - 1], send.at[step - 1], recv.at[step - 1], device(window, z, to, core)
        )

    for step in (2, 1, 3):
        for half in (1, 0):
            kv_copy(step, half).start()
    own = [
        pltpu.make_async_copy(kv_src.at[x, :, half], block_of(kv, half, z, x, core), own_sem.at[half])
        for half in (0, 1)
    ]

    def z_copy(gid, j, at, way, src=None):
        piece = piece_of(kv, gid, core, turn(x, -j))
        return remote(
            piece if src is None else src, piece,
            z_send.at[gid, (way + 1) // 2, j], z_recv.at[gid, j], device(window, at + way, x, core),
        )

    def next_copy(gid, j, src=None):
        piece = piece_of(kv, gid, core, turn(x, -j))
        return remote(
            piece if src is None else src, piece_of(kv, gid + 4, core, turn(x, -j)),
            next_send.at[j], next_recv.at[gid - 4, j], device(window + 1, 0, x, core),
        )

    def next_arrival(gid, j):
        piece = piece_of(kv, gid, core, turn(x, -j))
        return remote(piece, piece, next_send.at[j], next_recv.at[gid - 8, j], device(window, z, x, 1 - core))

    def core_copy(gid, j, src=None):
        piece = piece_of(kv, gid, core, turn(x, -j))
        return remote(
            piece if src is None else src, piece,
            core_send.at[gid, j], core_recv.at[gid, j], device(window, z, x, 1 - core),
        )

    def core_arrival(gid, j):
        piece = piece_of(kv, gid, 1 - core, turn(x, -j))
        return remote(piece, piece, core_send.at[gid, j], core_recv.at[gid, j], device(window, z, x, 1 - core))

    def level(at):
        def ways(gid):
            owner = 0 if gid >= 8 else owner_z(gid)
            return [
                way
                for way in (-1, 1)
                if 0 <= at + way < ZS and gid in NEED[at + way] and abs(at + way - owner) > abs(at - owner)
            ]

        def onward(gid, j, src=None):
            for way in ways(gid):
                z_copy(gid, j, at, way, src).start()
            core_copy(gid, j, src).start()

        def guarded(gid, act):
            if gid >= 8:
                pl.when(window > 0)(act)
            else:
                act()

        def given(j, src=False):
            for gid in (at + 4, at):
                first = kv_src.at[x, :, gid // 4] if src else None
                if gid >= 4 and at in PRIOR_FROM:
                    pl.when(window < WINDOWS - 1)(lambda: next_copy(gid, j, first).start())
                onward(gid, j, first)

        def arrived(gid, j):
            if gid >= 8 and at == 0:
                next_arrival(gid, j).wait_recv()
            else:
                z_copy(gid, j, at, 1 if at < ZS - 1 else -1).wait_recv()
            onward(gid, j)

        given(0, True)
        for copy in own:
            copy.start()
        for step in (2, 1, 3):
            wide(ld_src, ld, ld_send, ld_recv, step).start()
            wide(qd_src, qd, qd_send, qd_recv, step).start()

        @pl.loop(1, XS)
        def _(j):
            for half in (0, 1):
                kv_arrival(j, half).wait_recv()
            given(j)

        for gid in SPREAD_ORDER[at]:
            guarded(gid, lambda: pl.loop(0, XS)(lambda j: arrived(gid, j)))

        @pl.loop(0, XS)
        def _(j):
            for gid in NEED[at]:

                def act():
                    core_arrival(gid, j).wait_recv()
                    core_copy(gid, j).wait_send()
                    for way in ways(gid):
                        z_copy(gid, j, at, way).wait_send()

                guarded(gid, act)
            if at in PRIOR_FROM:
                pl.when(window < WINDOWS - 1)(lambda: next_copy(at + 4, j).wait_send())

    for at in range(ZS):
        pl.when(z == at)(lambda at=at: level(at))

    for copy in own:
        copy.wait()
    for step in (1, 2, 3):
        for half in (0, 1):
            kv_copy(step, half).wait_send()
        wide(ld_src, ld, ld_send, ld_recv, step).wait()
        wide(qd_src, qd, qd_send, qd_recv, step).wait()


def spread(kv_src, qd_src, ld_src):
    dma = pltpu.SemaphoreType.DMA
    anywhere = pl.BlockSpec(memory_space=pl.ANY)
    return pl.pallas_call(
        spread_kernel,
        out_shape=(
            jax.ShapeDtypeStruct((2, PAIRS, 2, BLK, DIM), jnp.bfloat16),
            jax.ShapeDtypeStruct((XS - 1, *qd_src.shape[1:]), jnp.bfloat16),
            jax.ShapeDtypeStruct((XS - 1, *ld_src.shape[1:]), jnp.float32),
        ),
        in_specs=[anywhere] * 3,
        out_specs=[anywhere] * 3,
        scratch_shapes=[
            dma((XS, 2)), dma((XS, 2)), dma((3,)), dma((3,)), dma((3,)), dma((3,)),
            dma((11, 2, XS)), dma((11, XS)), dma((XS,)), dma((3, XS)), dma((11, XS)), dma((11, XS)), dma((2,)),
        ],
        compiler_params=pltpu.CompilerParams(collective_id=0, has_side_effects=True),
        name="spread",
    )(kv_src, qd_src, ld_src)


def grads_kernel(
    info, starts, qd_own, ld_own, qd_a, ld_a, qd_b, ld_b, kv_hbm, dq, parts,
    kv, totals, dq_t, held, q, do, kv_sem,
):
    pair, half = pl.program_id(0), pl.program_id(1)
    window, z, core, x = info[0], info[1], info[2], info[3]
    slot_a, slot_b = (x - 2 * pair) & 3, (x - 2 * pair - 1) & 3

    @pl.when((pair == 0) & (half == 0))
    def _():
        load = pltpu.make_async_copy(kv_hbm, kv, kv_sem)
        load.start()
        totals[...] = jnp.zeros_like(totals)
        load.wait()

        def clear(first, blocks):
            kv[:, pl.ds(first * BLK, blocks * BLK), :] = jnp.zeros((2, blocks * BLK, DIM), jnp.bfloat16)

        clear(0, 2 * PAD_PAIRS)
        pl.when((z >= 2) | (window == 0))(lambda: clear(2 * PAD_PAIRS, 2 * PRIOR_PAIRS))
        pl.when(z == 0)(lambda: clear(2 * BASE_PAIRS + 8, 8))

    low = 8 * z + 4 * pair + core
    block_a = jnp.where(half == 0, low, WIN_BLOCKS - 1 - low)
    block_b = jnp.where(half == 0, low + 2, WIN_BLOCKS - 3 - low)
    shift = BASE_ROW - window * WIN_ROWS
    first = BASE_ROW + jnp.minimum(block_a, block_b) * BLK
    lane = lax.broadcasted_iota(jnp.int32, (1, 2 * ROWS), 1)
    query_row = BASE_ROW + jnp.where(lane < ROWS, block_a, block_b) * BLK + (lane & (BLK - 1))
    query_from = jnp.zeros((1, 2 * ROWS), jnp.int32)
    begin = 0
    for entry in range(24):
        at = starts[entry] + shift
        query_from = jnp.where(query_row >= at, at, query_from)
        begin = jnp.where(first >= at, at, begin)
    end = first + 3 * BLK
    tiles = (end - begin + TILE - 1) // TILE
    for at, slot, came in ((0, slot_a, qd_a), (ROWS, slot_b, qd_b)):
        q[pl.ds(at, ROWS), :] = jnp.where(slot == 0, qd_own[0], came[0])
        do[pl.ds(at, ROWS), :] = jnp.where(slot == 0, qd_own[1], came[1])

    def lanes_of(row):
        at = pl.ds(2 * half + row, 1)
        return jnp.concatenate(
            [jnp.where(slot == 0, ld_own[at, :], came[at, :]) for slot, came in ((slot_a, ld_a), (slot_b, ld_b))],
            axis=1,
        )

    lse, delta = lanes_of(0), lanes_of(1)
    dq_t[...] = jnp.zeros_like(dq_t)

    def scores(tile):
        row = pl.multiple_of(end - (tile + 1) * TILE, BLK)
        rows = pl.ds(row, TILE)
        s = lax.dot_general(kv[0, rows, :], q[...], (((1,), (1,)), ((), ())), preferred_element_type=jnp.float32)
        dp = lax.dot_general(kv[1, rows, :], do[...], (((1,), (1,)), ((), ())), preferred_element_type=jnp.float32)
        key_row = row + lax.broadcasted_iota(jnp.int32, (TILE, 1), 0)
        allowed = (key_row <= query_row) & (key_row >= query_from)
        p = jnp.where(allowed, jnp.exp2(s * (SCALE * LOG2E) - lse), 0.0)
        return p.astype(jnp.bfloat16), (p * (dp - delta)).astype(jnp.bfloat16)

    def products(tile, p, ds):
        rows = pl.ds(pl.multiple_of(end - (tile + 1) * TILE, BLK), TILE)
        totals[1, rows, :] += jnp.dot(p, do[...], preferred_element_type=jnp.float32)
        totals[0, rows, :] += jnp.dot(ds, q[...], preferred_element_type=jnp.float32)
        dq_t[...] += lax.dot_general(kv[0, rows, :], ds, (((0,), (0,)), ((), ())), preferred_element_type=jnp.float32)

    held[0], held[1] = scores(0)

    @pl.loop(1, tiles)
    def _(tile):
        p, ds = held[0], held[1]
        new_p, new_ds = scores(tile)
        products(tile - 1, p, ds)
        held[0], held[1] = new_p, new_ds

    products(tiles - 1, held[0], held[1])

    rows_out = (dq_t[...].T * SCALE).astype(jnp.bfloat16)
    dq[slot_a, half] = rows_out[:ROWS]
    dq[slot_b, half] = rows_out[ROWS:]

    @pl.when((pair == 1) & (half == 1))
    def _():
        parts[0] = (totals[0] * SCALE).astype(jnp.bfloat16)
        parts[1] = totals[1].astype(jnp.bfloat16)


def slot_at(info, pair, second):
    return jnp.maximum(((info[3] - 2 * pair - second) & 3) - 1, 0)


def grads(info, starts, qd_own, ld_own, qd, ld, kv):
    return pl.pallas_call(
        grads_kernel,
        grid_spec=pltpu.PrefetchScalarGridSpec(
            num_scalar_prefetch=2,
            grid=(2, 2),
            in_specs=[
                pl.BlockSpec((None, 2, None, ROWS, DIM), lambda s, h, info, _: (info[3], 0, h, 0, 0)),
                pl.BlockSpec((None, 8, ROWS), lambda s, h, info, _: (info[3], 0, 0)),
                *(
                    spec
                    for second in (0, 1)
                    for spec in (
                        pl.BlockSpec(
                            (None, 2, None, ROWS, DIM),
                            lambda s, h, info, _, second=second: (slot_at(info, s, second), 0, h, 0, 0),
                        ),
                        pl.BlockSpec(
                            (None, 8, ROWS),
                            lambda s, h, info, _, second=second: (slot_at(info, s, second), 0, 0),
                        ),
                    )
                ),
                pl.BlockSpec(memory_space=pl.ANY),
            ],
            out_specs=[
                pl.BlockSpec((XS, 2, ROWS, DIM), lambda s, h, *_: (0, 0, 0, 0)),
                pl.BlockSpec((2, KEY_ROWS, DIM), lambda s, h, *_: (0, 0, 0)),
            ],
            scratch_shapes=[
                pltpu.VMEM((2, KEY_ROWS, DIM), jnp.bfloat16),
                pltpu.VMEM((2, KEY_ROWS, DIM), jnp.float32),
                pltpu.VMEM((DIM, 2 * ROWS), jnp.float32),
                pltpu.VMEM((2, TILE, 2 * ROWS), jnp.bfloat16),
                pltpu.VMEM((2 * ROWS, DIM), jnp.bfloat16),
                pltpu.VMEM((2 * ROWS, DIM), jnp.bfloat16),
                pltpu.SemaphoreType.DMA,
            ],
        ),
        out_shape=(
            jax.ShapeDtypeStruct((XS, 2, ROWS, DIM), jnp.bfloat16),
            jax.ShapeDtypeStruct((2, KEY_ROWS, DIM), jnp.bfloat16),
        ),
        compiler_params=pltpu.CompilerParams(
            dimension_semantics=("arbitrary", "arbitrary"), vmem_limit_bytes=40 * 2**20
        ),
        name="grads",
    )(info, starts, qd_own, ld_own, qd, ld, qd, ld, kv)


def collect_kernel(
    dq_src, parts, dq, dkv, own, sib, stage, near, far, final,
    dq_send, dq_recv, own_sem, core_send, core_recv, z_send, z_recv, next_send, next_recv,
    out_send, out_recv, last_sem,
):
    window, z, x, core = place()
    greet(window, z, x, core)

    def core_copy(gid, j):
        return remote(
            piece_of(parts, gid, 1 - core, turn(x, j + 1)), sib.at[gid, j],
            core_send.at[gid, j], core_recv.at[gid, j], device(window, z, x, 1 - core),
        )

    def own_copy(gid, j):
        return pltpu.make_async_copy(piece_of(parts, gid, core, turn(x, j + 1)), own.at[gid, j], own_sem.at[gid, j])

    def dq_copy(step):
        to = turn(x, -step)
        return remote(
            dq_src.at[step], dq.at[x], dq_send.at[step - 1], dq_recv.at[step - 1], device(window, z, to, core)
        )

    def dq_arrival(step):
        came = turn(x, step)
        return remote(
            dq_src.at[step], dq.at[came], dq_send.at[step - 1], dq_recv.at[step - 1],
            device(window, z, came, core),
        )

    def out_copy(half, j):
        return remote(
            final.at[half, j], dkv.at[x, :, half],
            out_send.at[half, j], out_recv.at[half, j], device(window, z, turn(x, j + 1), core),
        )

    def out_arrival(half, j):
        came = turn(x, -j - 1)
        return remote(
            final.at[half, j], dkv.at[came, :, half],
            out_send.at[half, j], out_recv.at[half, j], device(window, z, came, core),
        )

    def out_own(half):
        return pltpu.make_async_copy(final.at[half, XS - 1], dkv.at[x, :, half], last_sem.at[1 + half])

    dq_own = pltpu.make_async_copy(dq_src.at[0], dq.at[x], last_sem.at[0])

    def z_copy(gid, j, at, way):
        return remote(
            stage.at[gid, j], near.at[gid, (1 - way) // 2, j],
            z_send.at[gid, j], z_recv.at[gid, (1 - way) // 2, j], device(window, at + way, x, core),
        )

    def next_copy(gid, j):
        return remote(
            stage.at[gid, j], far.at[j], next_send.at[gid - 8, j], next_recv.at[j],
            device(window - 1, owner_z(gid), x, core),
        )

    def next_arrival(j):
        return remote(
            stage.at[8, j], far.at[j], next_send.at[0, j], next_recv.at[j], device(window, z, x, 1 - core),
        )

    def level(at):
        order = COLLECT_ORDER[at]
        mine = (at, at + 4)

        def each(gids, act, j):
            for gid in gids:
                if gid >= 8:
                    pl.when(window > 0)(lambda: act(gid, j))
                else:
                    act(gid, j)

        def begin(gid, j):
            core_copy(gid, j).start()
            own_copy(gid, j).start()

        def towards(gid):
            owner = 0 if gid >= 8 else owner_z(gid)
            return 1 if owner > at else -1

        def summed(gid, j):
            own_copy(gid, j).wait()
            core_copy(gid, j).wait_recv()
            total = own[gid, j].astype(jnp.float32) + sib[gid, j].astype(jnp.float32)
            owner = 0 if gid >= 8 else owner_z(gid)
            for way in (-1, 1):
                came = at + way
                if 0 <= came < ZS and gid in NEED[came] and abs(came - owner) > abs(at - owner):
                    z_copy(gid, j, came, -way).wait_recv()
                    total = total + near[gid, (way + 1) // 2, j].astype(jnp.float32)
            return total

        def pass_on(gid, j):
            stage[gid, j] = summed(gid, j).astype(jnp.bfloat16)
            if gid >= 8 and at == 0:
                next_copy(gid, j).start()
            else:
                z_copy(gid, j, at, towards(gid)).start()

        def keep(half, j):
            total = summed(mine[half], j)
            if half == 0 or at not in PRIOR_FROM:
                final[half, j] = total.astype(jnp.bfloat16)
            else:

                @pl.when(window < WINDOWS - 1)
                def _():
                    next_arrival(j).wait_recv()
                    final[half, j] = (total + far[j].astype(jnp.float32)).astype(jnp.bfloat16)

                @pl.when(window == WINDOWS - 1)
                def _():
                    final[half, j] = total.astype(jnp.bfloat16)

        def finish(gid, j):
            core_copy(gid, j).wait_send()
            if gid in mine:
                return
            if gid >= 8 and at == 0:
                next_copy(gid, j).wait_send()
            else:
                z_copy(gid, j, at, towards(gid)).wait_send()

        for gid in (*order, *mine):
            each([gid], lambda gid, _: pl.loop(0, XS)(lambda j: begin(gid, j)), None)

        dq_own.start()
        for step in (2, 1, 3):
            dq_copy(step).start()
        for gid in order:
            each([gid], lambda gid, _: pl.loop(0, XS)(lambda j: pass_on(gid, j)), None)
        for half in (0, 1):

            @pl.loop(0, XS - 1)
            def _(j):
                keep(half, j)
                out_copy(half, j).start()

            keep(half, XS - 1)
            out_own(half).start()

        @pl.loop(0, XS)
        def _(j):
            each((*order, *mine), finish, j)

    for at in range(ZS):
        pl.when(z == at)(lambda at=at: level(at))

    dq_own.wait()
    for half in (0, 1):
        out_own(half).wait()
    for step in (1, 2, 3):
        dq_arrival(step).wait_recv()
        dq_copy(step).wait_send()
        for half in (0, 1):
            out_arrival(half, step - 1).wait_recv()
            out_copy(half, step - 1).wait_send()


def collect(dq_src, parts):
    dma = pltpu.SemaphoreType.DMA
    anywhere = pl.BlockSpec(memory_space=pl.ANY)
    piece = (2, BLK, DIM)
    return pl.pallas_call(
        collect_kernel,
        out_shape=(
            jax.ShapeDtypeStruct(dq_src.shape, jnp.bfloat16),
            jax.ShapeDtypeStruct((XS, 2, 2, BLK, DIM), jnp.bfloat16),
        ),
        in_specs=[anywhere] * 2,
        out_specs=[anywhere] * 2,
        scratch_shapes=[
            pltpu.VMEM((11, XS, *piece), jnp.bfloat16),
            pltpu.VMEM((11, XS, *piece), jnp.bfloat16),
            pltpu.VMEM((11, XS, *piece), jnp.bfloat16),
            pltpu.VMEM((11, 2, XS, *piece), jnp.bfloat16),
            pltpu.VMEM((XS, *piece), jnp.bfloat16),
            pltpu.VMEM((2, XS, *piece), jnp.bfloat16),
            dma((3,)), dma((3,)), dma((11, XS)), dma((11, XS)), dma((11, XS)), dma((11, XS)), dma((11, 2, XS)),
            dma((3, XS)), dma((XS,)), dma((2, XS)), dma((2, XS)), dma((3,)),
        ],
        compiler_params=pltpu.CompilerParams(
            collective_id=1, has_side_effects=True, vmem_limit_bytes=32 * 2**20
        ),
        name="collect",
    )(dq_src, parts)


def by_head(rows):
    cut = rows.reshape(2, BLK, KV, GROUP, DIM).transpose(2, 0, 3, 1, 4)
    return cut.reshape(KV, 2, ROWS, DIM)


def lanes(rows):
    return rows.reshape(KV, GROUP, 2, BLK).transpose(0, 2, 1, 3).reshape(KV, 2, ROWS)


def on_device(query, key, value, output, grad_output, lse, doc_starts):
    window, z, x, core = place()
    delta = jnp.einsum("qhd,qhd->hq", grad_output, output, preferred_element_type=jnp.float32)
    rows = jnp.stack([lanes(lse * LOG2E), lanes(delta)], axis=2).reshape(KV, 4, ROWS)
    ld_src = jnp.concatenate([rows, jnp.zeros_like(rows)], axis=1)
    qd_src = jnp.stack([by_head(query), by_head(grad_output)], axis=1)
    kv_src = jnp.stack([key, value]).reshape(2, 2, BLK, KV, DIM).transpose(3, 0, 1, 2, 4)
    kv, qd, ld = spread(kv_src, qd_src, ld_src)
    info = jnp.stack([window, z, core, x]).astype(jnp.int32)
    dq, parts = grads(info, doc_starts, qd_src, ld_src, qd, ld, kv.reshape(2, KEY_ROWS, DIM))
    dq_back, dkv = collect(dq, parts.reshape(2, PAIRS, 2, BLK, DIM))
    grad_query = (
        dq_back.reshape(KV, 2, GROUP, BLK, DIM).transpose(1, 3, 0, 2, 4).reshape(2 * BLK, KV * GROUP, DIM)
    )
    back = dkv.transpose(1, 2, 3, 0, 4).reshape(2, 2 * BLK, KV, DIM)
    return grad_query, back[0], back[1]


def solution(mesh):
    tokens = P(("outer", "inner"), None, None)
    return jax.shard_map(
        on_device,
        mesh=mesh,
        in_specs=(tokens, tokens, tokens, tokens, tokens, P(None, ("outer", "inner")), P()),
        out_specs=(tokens, tokens, tokens),
        check_vma=False,
    )
```
